256 devices in a mesh: node: 64 (over y, z_hi, x, core), local: 4 (over z_lo).
Axes of the slice: x: 4, y: 4, z: 8 (z_hi: 2, z_lo: 4; z = z_hi * 4 + z_lo), core: 2. Of those that a mesh axis runs over, the one named last changes fastest.
Arguments:
- tokens: bfloat16 [65536, 4096], P(('node', 'local')), may hold values from -24 to 24
- queries: bfloat16 [65536, 4096], P(('node', 'local')), may hold values from -240 to 240
- values: bfloat16 [65536, 512], P(('node', 'local')), may hold values from -6 to 6
- upstream: bfloat16 [65536, 4096], P(('node', 'local')), may hold values from -6 to 6
- key_weight: bfloat16 [4096, 512], P(('node', 'local')), may hold values from -0.09375 to 0.09375
- positions: int32 [65536], P(('node', 'local')), may hold values from 0 to 255, as said below
Outputs:
- grad_tokens: bfloat16 [65536, 4096], P(('node', 'local'))
- grad_weight: float32 [4096, 512], P(('node', 'local'))
The draws below stay inside these ranges and needn't reach their ends.
Inputs may be any that keep to these rules, and one draw needn't show every extreme that they name: positions[i] counts the earlier tokens of token i's document; every block of 256 rows starts a document, and no document crosses such a block.
All inputs are finite; a program needn't handle non-finite values.
Results may differ from the reference program's by a relative error of at most 0.033.
Values may be sent and summed in bfloat16 or wider, within the bound.
A program may use at most 128 MiB of HBM per device.

```python
import jax
import jax.numpy as jnp
from jax import lax

D = 4096
KEY_VALUE_HEADS = 4
GROUP = 8
HEAD_SIZE = 128
TOK_DEV = 256
HEADS = 32
KEY_WIDTH = 512
TOKENS = 65536


def draw_queries(key, part):
    width = HEADS * HEAD_SIZE
    base = jax.random.normal(key, (TOKENS, width), jnp.float32)
    return jnp.clip(base, -240.0, 240.0).astype(jnp.bfloat16)


def draw_positions(key, part):
    first_key, second_key = jax.random.split(jax.random.fold_in(key, 11))
    place = jnp.arange(TOKENS, dtype=jnp.int32)
    starts = jax.random.randint(first_key, (TOKENS,), 0, 48) == 0
    single = jax.random.randint(second_key, (), 0, TOKENS // TOK_DEV)
    starts = starts & (place // TOK_DEV != single) | (place % TOK_DEV == 0)
    marks = jnp.where(starts, place, 0)
    latest = lax.cummax(marks, axis=0)
    return (place - latest).astype(jnp.int32)


def with_spikes(values, stream_key, source, target, shards_of, factor):
    def block_of(position):
        return (jnp.arange(values.shape[position]) // (values.shape[position] // shards_of)).reshape((-1,) + (1,) * (values.ndim - 1 - position))

    first = jax.random.permutation(stream_key, shards_of)[block_of(target)]
    far = (block_of(target) + shards_of // 2) % shards_of
    return jnp.where((block_of(source) == first) | (block_of(source) == far), factor * values, values)


def block_scale(own_key, shape, pieces, low, top_value):
    def one(dim, shards_of):
        heights = jax.random.uniform(jax.random.fold_in(jax.random.fold_in(own_key, 6), dim), (shards_of,), jnp.float32, low / len(pieces), top_value / len(pieces))
        return jnp.repeat(jnp.exp(heights), shape[dim] // shards_of).reshape((-1,) + (1,) * (len(shape) - dim - 1))

    level = one(*pieces[0])
    for cut in pieces[1:]:
        level = level * one(*cut)
    return level


def noise(stream_key, dims, spread, limit, pieces=(), kind=jnp.bfloat16):
    drawn = jax.random.normal(stream_key, dims, jnp.float32) * spread
    if len(pieces) > 0:
        drawn = block_scale(stream_key, dims, pieces, -0.22, 0.18) * drawn
    return jnp.clip(drawn, min=-limit, max=limit).astype(kind)


def bell_draw_with(own_key, shape, deviation, limit, shards, heavy, held_as=jnp.bfloat16):
    entries = deviation * jax.random.normal(own_key, shape, jnp.float32)
    if shards:
        entries = entries * block_scale(own_key, shape, shards, -0.22, 0.18)
    return jnp.clip(with_spikes(entries, jax.random.fold_in(own_key, 3), *heavy), -limit, limit).astype(held_as)


def setup_inputs(seed: int = 0) -> dict:
    arg_keys = jax.random.split(jax.random.key(seed), 7)
    return {
        "tokens": bell_draw_with(arg_keys[0], (TOKENS, D), 1.0, 24.0, ((0, 256),), (0, 1, 256, 6.0)),
        "queries": draw_queries(jax.random.fold_in(arg_keys[6], 71), 0),
        "values": noise(arg_keys[2], (TOKENS, KEY_WIDTH), 1.0, 6.0, ((0, 256),)),
        "upstream": noise(arg_keys[3], (TOKENS, HEADS * HEAD_SIZE), 1.0, 6.0, ((0, 256),)),
        "key_weight": noise(arg_keys[4], (D, KEY_WIDTH), D ** -0.5, 0.09375, ((0, 256),)),
        "positions": draw_positions(jax.random.fold_in(arg_keys[6], 71), 0),
    }


def angle_tables(positions):
    half = HEAD_SIZE // 2
    freq = jnp.exp(-(jnp.arange(half, dtype=jnp.float32) * 2.0 / HEAD_SIZE) * jnp.log(jnp.float32(1000000.0)))
    angle = positions.astype(jnp.float32)[:, None] * freq[None, :]
    return jnp.cos(angle)[:, None, :], jnp.sin(angle)[:, None, :]


def rotate(raw_keys, cosine, sine_part):
    shaped = raw_keys.reshape(raw_keys.shape[0], KEY_VALUE_HEADS, HEAD_SIZE)
    half = HEAD_SIZE // 2
    first, second = shaped[..., :half], shaped[..., half:]
    joined = jnp.concatenate([first * cosine - second * sine_part, second * cosine + first * sine_part], axis=-1)
    return joined.reshape(raw_keys.shape[0], KEY_VALUE_HEADS * HEAD_SIZE)


def unrotate(grad_rot, cosine, sine_part):
    shaped = grad_rot.reshape(grad_rot.shape[0], KEY_VALUE_HEADS, HEAD_SIZE)
    half = HEAD_SIZE // 2
    first, second = shaped[..., :half], shaped[..., half:]
    joined = jnp.concatenate([first * cosine + second * sine_part, second * cosine - first * sine_part], axis=-1)
    return joined.reshape(grad_rot.shape[0], KEY_VALUE_HEADS * HEAD_SIZE)


def attend_back(queries, keys, values, upstream, positions):
    item_count = queries.shape[0]
    scale = HEAD_SIZE ** -0.5
    qmat = queries.reshape(item_count, KEY_VALUE_HEADS, GROUP, HEAD_SIZE).astype(jnp.float32)
    kmat = keys.reshape(item_count, KEY_VALUE_HEADS, HEAD_SIZE).astype(jnp.float32)
    value_matrix = values.reshape(item_count, KEY_VALUE_HEADS, HEAD_SIZE).astype(jnp.float32)
    upper_matrix = upstream.reshape(item_count, KEY_VALUE_HEADS, GROUP, HEAD_SIZE).astype(jnp.float32)
    scores = jnp.einsum('yxru,oxu->xryo', qmat, kmat) * scale
    place = jnp.arange(item_count, dtype=jnp.int32)
    allowed = (place[None, :] <= place[:, None]) & (place[None, :] >= (place - positions)[:, None])
    scores = jnp.where(allowed, scores, jnp.float32(-1e30))
    top = jnp.max(scores, axis=-1, keepdims=True)
    expo = jnp.exp(scores - top)
    probs = expo / jnp.sum(expo, axis=-1, keepdims=True)
    slope_values = jnp.einsum('yxru,oxu->xryo', upper_matrix, value_matrix)
    inner = jnp.sum(probs * slope_values, axis=-1, keepdims=True)
    dscores = (probs * (slope_values - inner) * scale).astype(jnp.bfloat16)
    grad_rot = jnp.einsum('kgts,tkgd->skd', dscores.astype(jnp.float32), qmat)
    return grad_rot.reshape(item_count, KEY_VALUE_HEADS * HEAD_SIZE)


def reference(tokens, queries, values, upstream, key_weight, positions):
    raw_keys = jnp.dot(tokens, key_weight, preferred_element_type=jnp.float32)
    cosine, sine_part = angle_tables(positions)
    keys = rotate(raw_keys, cosine, sine_part).astype(jnp.bfloat16)
    blocks = TOKENS // TOK_DEV

    def one_block(item):
        qblk, kblk, vblk, ublk, pblk, cblk, sblk = item
        grad_rot = attend_back(qblk, kblk, vblk, ublk, pblk)
        return unrotate(grad_rot, cblk, sblk).astype(jnp.bfloat16)

    items = (queries.reshape(blocks, TOK_DEV, -1), keys.reshape(blocks, TOK_DEV, -1),
             values.reshape(blocks, TOK_DEV, -1), upstream.reshape(blocks, TOK_DEV, -1),
             positions.reshape(blocks, TOK_DEV), cosine.reshape(blocks, TOK_DEV, 1, -1),
             sine_part.reshape(blocks, TOK_DEV, 1, -1))
    grad_keys = lax.map(one_block, items).reshape(TOKENS, KEY_VALUE_HEADS * HEAD_SIZE)
    grad_tokens = lax.dot_general(grad_keys, key_weight, (((1,), (1,)), ((), ())),
                                  preferred_element_type=jnp.float32).astype(jnp.bfloat16)
    grad_weight = lax.dot_general(tokens, grad_keys, (((0,), (0,)), ((), ())),
                                  preferred_element_type=jnp.float32)
    return grad_tokens, grad_weight
```

```python
import math

import jax
import jax.numpy as jnp
from jax import lax
from jax.experimental import pallas as pl
from jax.experimental.pallas import tpu as pltpu
from jax.sharding import Mesh
from jax.sharding import PartitionSpec as P

AXES = ("y", "zh", "x", "c", "zl")
MESH = pl.DeviceIdType.MESH
HEADS = 4
GROUP = 8
HEAD = 128
TOK = 256
D = 4096
SCALE = HEAD**-0.5
BF = jnp.bfloat16
F32 = jnp.float32
NT = (((1,), (1,)), ((), ()))


def dot_nt(a, b):
    return lax.dot_general(a, b, NT, preferred_element_type=F32)


def dot(a, b):
    return jnp.dot(a, b, preferred_element_type=F32)


def kernel(
    tok_hbm, q_hbm, v_hbm, u_hbm, kw_hbm, pos_hbm,
    gt_hbm, gw_out,
    tok, q, v, u, kw, pos, W, TT, cosine, sine, bias, keys, acc, gk, gt,
    own, other, RC, A, RAE, RAO, B, RB, C, RZ,
    load_sem, store_sem,
    zs, zr, s1s, s1r, s2s, s2r, cs, cr,
    rcs, rcr, ras, rar, rbs, rbr, rzs, rzr,
):
    y, zh, x, c, zl = (lax.axis_index(a) for a in AXES)
    z = zh * 4 + zl
    other_core = (y, zh, x, 1 - c, zl)

    def at_x(k):
        return (y, zh, lax.rem(x + k, 4), c, zl)

    def at_y(k):
        return (lax.rem(y + k, 4), zh, x, c, zl)

    def at_z(k):
        there = lax.rem(z + k, 8)
        return (y, there // 4, x, c, lax.rem(there, 4))

    def send(src, dst, send_sem, recv_sem, where):
        pltpu.make_async_remote_copy(
            src_ref=src, dst_ref=dst, send_sem=send_sem, recv_sem=recv_sem,
            device_id=where, device_id_type=MESH,
        ).start()

    def wait(like, sem):
        pltpu.make_async_copy(like, like, sem).wait()

    loads = [(kw_hbm, kw), (pos_hbm, pos), (tok_hbm, tok), (v_hbm, v), (q_hbm, q), (u_hbm, u)]
    copies = [pltpu.make_async_copy(a, b, load_sem.at[i]) for i, (a, b) in enumerate(loads)]
    for copy in copies:
        copy.start()
    barrier = pltpu.get_barrier_semaphore()
    peers = [other_core] + [at_x(k) for k in (1, 2, 3)] + [at_y(k) for k in (1, 2, 3)]
    peers += [at_z(k) for k in range(1, 8)]
    for peer in peers:
        pl.semaphore_signal(barrier, inc=1, device_id=peer, device_id_type=MESH)
    copies[0].wait()
    for h in range(HEADS):
        W[h, y, zh, x, c, zl] = kw[:, h * HEAD : (h + 1) * HEAD]
    pl.semaphore_wait(barrier, len(peers))

    mine = W.at[:, y, zh, x, c, zl]
    for k in range(1, 8):
        send(mine, mine, zs.at[k - 1], zr.at[k - 1], at_z(k))

    copies[1].wait()
    lane = lax.broadcasted_iota(jnp.int32, (1, HEAD), 1)
    half = HEAD // 2
    freq = jnp.exp(-(lax.rem(lane, half).astype(F32) * 2.0 / HEAD) * math.log(1000000.0))
    place = pos[...].astype(F32)
    column = jnp.broadcast_to(place, (HEAD, TOK)).T
    angle = column * freq
    cosine[...] = jnp.cos(angle)
    sine[...] = jnp.where(lane < half, -1.0, 1.0) * jnp.sin(angle)
    row = lax.broadcasted_iota(jnp.int32, (TOK, TOK), 0)
    col = lax.broadcasted_iota(jnp.int32, (TOK, TOK), 1)
    allowed = (row <= col) & (row >= col - pos[...])
    bias[...] = jnp.where(allowed, 0.0, -1e30).astype(F32)

    copies[2].wait()

    def turn(i, _):
        block = tok[:, pl.ds(pl.multiple_of(i * HEAD, HEAD), HEAD)].T
        TT[c, i] = block[:64]
        TT[1 - c, i] = block[64:]
        return 0

    lax.fori_loop(0, 32, turn, 0)

    for k in range(1, 8):
        wait(mine, zr.at[k - 1])

    def first_slice(h):
        return W.at[h, y, :, x, c]

    def second_slice(h):
        return W.at[h, y, :, :, c] if h % 2 == 0 else W.at[h, :, :, x, c]

    def core_slice(h):
        return W.at[h, :, :, :, c]

    for h in range(HEADS):
        for k in (1, 2, 3):
            piece = first_slice(h)
            send(piece, piece, s1s.at[h, k - 1], s1r.at[h, k - 1], at_x(k) if h % 2 == 0 else at_y(k))
    for copy in copies[3:]:
        copy.wait()
    for h in range(HEADS):
        for k in (1, 2, 3):
            wait(first_slice(h), s1r.at[h, k - 1])
        for k in (1, 2, 3):
            piece = second_slice(h)
            send(piece, piece, s2s.at[h, k - 1], s2r.at[h, k - 1], at_y(k) if h % 2 == 0 else at_x(k))

    def to_core(h):
        for k in (1, 2, 3):
            wait(second_slice(h), s2r.at[h, k - 1])
        send(core_slice(h), core_slice(h), cs.at[h], cr.at[h], other_core)

    def r0(h):
        send(other.at[h], RC.at[h], rcs.at[h], rcr.at[h], other_core)

    def a_slice(h, k):
        if h % 2 == 0:
            return A.at[h, lax.rem(y + k, 4)]
        return A.at[h, :, :, lax.rem(x + k, 4)]

    def b_slice(h, k):
        if h % 2 == 0:
            return B.at[h, :, lax.rem(x + k, 4)]
        return B.at[h, :, lax.rem(y + k, 4)]

    def ra_slot(h, k):
        return (RAO if h % 2 else RAE).at[h // 2, k - 1]

    def r1(h):
        wait(RC.at[h], rcr.at[h])

        def add(i, _):
            A[h, i] = (own[h, i] + RC[h, i].astype(F32)).astype(BF)
            return 0

        lax.fori_loop(0, 4, add, 0)
        for k in (1, 2, 3):
            send(a_slice(h, k), ra_slot(h, k), ras.at[h, k - 1], rar.at[h, k - 1], at_y(k) if h % 2 == 0 else at_x(k))

    def r2(h):
        for k in (1, 2, 3):
            wait(ra_slot(h, k), rar.at[h, k - 1])
        for i in range(2):
            for j in range(4):
                if h % 2 == 0:
                    total = A[h, y, i, j].astype(F32)
                    for k in range(3):
                        total = total + RAE[h // 2, k, i, j].astype(F32)
                else:
                    total = A[h, j, i, x].astype(F32)
                    for k in range(3):
                        total = total + RAO[h // 2, k, j, i].astype(F32)
                B[h, i, j] = total
        for k in (1, 2, 3):
            send(b_slice(h, k), RB.at[h, k - 1], rbs.at[h, k - 1], rbr.at[h, k - 1], at_x(k) if h % 2 == 0 else at_y(k))

    def r3(h):
        for k in (1, 2, 3):
            wait(RB.at[h, k - 1], rbr.at[h, k - 1])
        me = x if h % 2 == 0 else y
        for i in range(2):
            total = B[h, i, me]
            for k in range(3):
                total = total + RB[h, k, i]
            C[h, i] = total.reshape(4, 16, HEAD)
        for k in range(1, 8):
            there = lax.rem(z + k, 8)
            send(C.at[h, there // 4, lax.rem(there, 4)], RZ.at[h, k - 1], rzs.at[h, k - 1], rzr.at[h, k - 1], at_z(k))

    def r4(h):
        for k in range(1, 8):
            wait(RZ.at[h, k - 1], rzr.at[h, k - 1])
        total = C[h, zh, zl]
        for k in range(7):
            total = total + RZ[h, k]
        gw_out[:, h * HEAD : (h + 1) * HEAD] = total

    def project(h):
        wait(core_slice(h), cr.at[h])
        total = jnp.zeros((TOK, HEAD), F32)
        for i in range(4):
            total = total + dot(tok[:, i * 1024 : (i + 1) * 1024], W[h, i].reshape(1024, HEAD))
        keys[...] = (total * cosine[...] + pltpu.roll(total, half, 1) * sine[...]).astype(BF)

    def attend(h):
        acc[...] = jnp.zeros_like(acc)

        def one(g, _):
            lanes = pl.ds(pl.multiple_of((h * GROUP + g) * HEAD, HEAD), HEAD)
            queries = q[:, lanes]
            upper = u[:, lanes]
            scores = dot_nt(keys[...], queries)
            slopes = dot_nt(v[:, h * HEAD : (h + 1) * HEAD], upper)
            parts = []
            for b in range(2):
                n = (b + 1) * 128
                span = slice(b * 128, (b + 1) * 128)
                s = scores[:n, span] + bias[:n, span]
                top = jnp.max(s, axis=0, keepdims=True)
                expo = jnp.exp((s - top) * SCALE)
                sl = slopes[:n, span]
                norm = 1.0 / jnp.sum(expo, axis=0, keepdims=True)
                inner = jnp.sum(expo * sl, axis=0, keepdims=True) * norm
                parts.append((expo * (sl - inner) * (norm * SCALE)).astype(BF))
            low = jnp.concatenate([parts[0], jnp.zeros((128, 128), BF)], axis=0)
            dscores = jnp.concatenate([low, parts[1]], axis=1)
            acc[...] += dot(dscores, queries)
            return 0

        lax.fori_loop(0, GROUP, one, 0)

    def weight(h):
        total = acc[...]
        mine = (total * cosine[...] - pltpu.roll(total, half, 1) * sine[...]).astype(BF)
        gk[:, h * HEAD : (h + 1) * HEAD] = mine

        def give(i, _):
            eight = pl.ds(pl.multiple_of(i * 8, 8), 8)
            given = dot(TT[1, eight].reshape(512, TOK), mine)
            other[h, i] = given.astype(BF).reshape(2, 4, 64, HEAD)
            return 0

        lax.fori_loop(0, 4, give, 0)
        r0(h)

        def keep(i, _):
            eight = pl.ds(pl.multiple_of(i * 8, 8), 8)
            own[h, i] = dot(TT[0, eight].reshape(512, TOK), mine).reshape(2, 4, 64, HEAD)
            return 0

        lax.fori_loop(0, 4, keep, 0)

    def tokens_part(i):
        def one(n, _):
            rows = [W[h, n // 2, n % 2].reshape(512, HEAD) for h in range(HEADS)]
            cols = pl.ds(pl.multiple_of(n * 512, 512), 512)
            gt[:, cols] = dot_nt(gk[...], jnp.concatenate(rows, axis=1)).astype(BF)
            return 0

        lax.fori_loop(2 * i, 2 * i + 2, one, 0)
        cols = pl.ds(i * 1024, 1024)
        pltpu.make_async_copy(gt.at[:, cols], gt_hbm.at[:, cols], store_sem.at[i]).start()

    to_core(0)
    to_core(1)
    for h in range(HEADS):
        project(h)
        if h + 2 < HEADS:
            to_core(h + 2)
        attend(h)
        if h >= 1:
            r1(h - 1)
        weight(h)
        if h >= 2:
            r2(h - 2)
        if h >= 3:
            r3(h - 3)
    tokens_part(0)
    r1(3)
    r2(2)
    r3(1)
    tokens_part(1)
    tokens_part(2)
    r2(3)
    r3(2)
    r4(0)
    r4(1)
    tokens_part(3)
    r3(3)
    r4(2)
    r4(3)

    for k in range(7):
        wait(mine, zs.at[k])
    for h in range(HEADS):
        for k in range(3):
            wait(first_slice(h), s1s.at[h, k])
            wait(second_slice(h), s2s.at[h, k])
            wait(ra_slot(h, k + 1), ras.at[h, k])
            wait(RB.at[h, k], rbs.at[h, k])
        wait(core_slice(h), cs.at[h])
        wait(RC.at[h], rcs.at[h])
        for k in range(7):
            wait(RZ.at[h, k], rzs.at[h, k])
    for i in range(4):
        cols = pl.ds(i * 1024, 1024)
        wait(gt_hbm.at[:, cols], store_sem.at[i])


def per_device(tokens, queries, values, upstream, key_weight, positions):
    anywhere = pl.BlockSpec(memory_space=pl.ANY)
    dma = pltpu.SemaphoreType.DMA
    vm = pltpu.VMEM
    return pl.pallas_call(
        kernel,
        out_shape=(jax.ShapeDtypeStruct((TOK, D), BF), jax.ShapeDtypeStruct((16, HEADS * HEAD), F32)),
        in_specs=[anywhere] * 6,
        out_specs=(anywhere, pl.BlockSpec(memory_space=pltpu.VMEM)),
        scratch_shapes=[
            vm((TOK, D), BF), vm((TOK, D), BF), vm((TOK, HEADS * HEAD), BF), vm((TOK, D), BF),
            vm((16, HEADS * HEAD), BF), vm((1, TOK), jnp.int32),
            vm((HEADS, 4, 2, 4, 2, 4, 16, HEAD), BF),
            vm((2, 32, 64, TOK), BF),
            vm((TOK, HEAD), F32), vm((TOK, HEAD), F32), vm((TOK, TOK), F32),
            vm((TOK, HEAD), BF), vm((TOK, HEAD), F32), vm((TOK, HEADS * HEAD), BF), vm((TOK, D), BF),
            vm((HEADS, 4, 2, 4, 64, HEAD), F32),
            vm((HEADS, 4, 2, 4, 64, HEAD), BF),
            vm((HEADS, 4, 2, 4, 64, HEAD), BF),
            vm((HEADS, 4, 2, 4, 64, HEAD), BF),
            vm((2, 3, 2, 4, 64, HEAD), BF), vm((2, 3, 4, 2, 64, HEAD), BF),
            vm((HEADS, 2, 4, 64, HEAD), F32),
            vm((HEADS, 3, 2, 64, HEAD), F32),
            vm((HEADS, 2, 4, 16, HEAD), F32),
            vm((HEADS, 7, 16, HEAD), F32),
            dma((6,)), dma((4,)),
            dma((7,)), dma((7,)), dma((HEADS, 3)), dma((HEADS, 3)), dma((HEADS, 3)), dma((HEADS, 3)),
            dma((HEADS,)), dma((HEADS,)),
            dma((HEADS,)), dma((HEADS,)), dma((HEADS, 3)), dma((HEADS, 3)), dma((HEADS, 3)), dma((HEADS, 3)),
            dma((HEADS, 7)), dma((HEADS, 7)),
        ],
        compiler_params=pltpu.CompilerParams(
            collective_id=0, has_side_effects=True, vmem_limit_bytes=56 << 20
        ),
        cost_estimate=pl.CostEstimate(
            flops=5_000_000_000, bytes_accessed=9_000_000, transcendentals=2_000_000
        ),
        name="key_backward",
    )(tokens, queries, values, upstream, key_weight, positions.reshape(1, TOK))


def solution(mesh):
    torus = Mesh(mesh.devices.reshape(4, 2, 4, 2, mesh.shape["local"]), AXES)
    rows = P(AXES, None)
    return jax.shard_map(
        per_device,
        mesh=torus,
        in_specs=(rows, rows, rows, rows, rows, P(AXES)),
        out_specs=(rows, rows),
        check_vma=False,
    )
```

```python
import math

import jax
import jax.numpy as jnp
from jax import lax
from jax.experimental import pallas as pl
from jax.experimental.pallas import tpu as pltpu
from jax.sharding import Mesh
from jax.sharding import PartitionSpec as P

AXES = ("y", "zh", "x", "c", "zl")
MESH = pl.DeviceIdType.MESH
HEADS = 4
GROUP = 8
HEAD = 128
TOK = 256
D = 4096
SCALE = HEAD**-0.5
BF = jnp.bfloat16
F32 = jnp.float32
NT = (((1,), (1,)), ((), ()))


def dot_nt(a, b):
    return lax.dot_general(a, b, NT, preferred_element_type=F32)


def dot(a, b):
    return jnp.dot(a, b, preferred_element_type=F32)


def kernel(
    tok_hbm, q_hbm, v_hbm, u_hbm, kw_hbm, pos_hbm,
    gt, gw_out,
    SL, tok, q, v, u, kw, pos, W, TT, cosine, sine, bias, keys, acc, gk,
    own, other, RC, A, RA, B, RB, C, RZ,
    load_sem,
    zs, zr, s1s, s1r, s2s, s2r, cs, cr,
    rcs, rcr, ras, rar, rbs, rbr, rzs, rzr,
):
    y, zh, x, c, zl = (lax.axis_index(a) for a in AXES)
    z = zh * 4 + zl
    other_core = (y, zh, x, 1 - c, zl)

    def at_x(k):
        return (y, zh, lax.rem(x + k, 4), c, zl)

    def at_y(k):
        return (lax.rem(y + k, 4), zh, x, c, zl)

    def at_z(k):
        there = lax.rem(z + k, 8)
        return (y, there // 4, x, c, lax.rem(there, 4))

    def send(src, dst, send_sem, recv_sem, where):
        pltpu.make_async_remote_copy(
            src_ref=src, dst_ref=dst, send_sem=send_sem, recv_sem=recv_sem,
            device_id=where, device_id_type=MESH,
        ).start()

    def wait(like, sem):
        pltpu.make_async_copy(like, like, sem).wait()

    loads = [(kw_hbm, kw), (pos_hbm, pos), (tok_hbm, tok), (v_hbm, v), (q_hbm, q), (u_hbm, u)]
    copies = [pltpu.make_async_copy(a, b, load_sem.at[i]) for i, (a, b) in enumerate(loads)]
    for copy in copies:
        copy.start()
    barrier = pltpu.get_barrier_semaphore()
    peers = [other_core] + [at_x(k) for k in (1, 2, 3)] + [at_y(k) for k in (1, 2, 3)]
    peers += [at_z(k) for k in range(1, 8)]
    for peer in peers:
        pl.semaphore_signal(barrier, inc=1, device_id=peer, device_id_type=MESH)
    copies[0].wait()
    for h in range(HEADS):
        W[h, y, zh, x, c, zl] = kw[:, h * HEAD : (h + 1) * HEAD]
    pl.semaphore_wait(barrier, len(peers))

    mine = W.at[:, y, zh, x, c, zl]
    for k in range(1, 8):
        send(mine, mine, zs.at[k - 1], zr.at[k - 1], at_z(k))

    copies[1].wait()
    lane = lax.broadcasted_iota(jnp.int32, (1, HEAD), 1)
    half = HEAD // 2
    freq = jnp.exp(-(lax.rem(lane, half).astype(F32) * 2.0 / HEAD) * math.log(1000000.0))
    place = pos[...].astype(F32)
    column = jnp.broadcast_to(place, (HEAD, TOK)).T
    angle = column * freq
    cosine[...] = jnp.cos(angle)
    sine[...] = jnp.where(lane < half, -1.0, 1.0) * jnp.sin(angle)
    row = lax.broadcasted_iota(jnp.int32, (TOK, TOK), 0)
    col = lax.broadcasted_iota(jnp.int32, (TOK, TOK), 1)
    allowed = (row <= col) & (row >= col - pos[...])
    bias[...] = jnp.where(allowed, 0.0, -1e30).astype(F32)

    copies[2].wait()

    def turn(i, _):
        block = tok[:, pl.ds(pl.multiple_of(i * HEAD, HEAD), HEAD)].T
        TT[c, i] = block[:64]
        TT[1 - c, i] = block[64:]
        return 0

    lax.fori_loop(0, 32, turn, 0)

    for k in range(1, 8):
        wait(mine, zr.at[k - 1])

    def slopes(h):
        def one(g, _):
            n = h * GROUP + g
            upper = u[:, pl.ds(pl.multiple_of(n * HEAD, HEAD), HEAD)]
            full = dot_nt(v[:, h * HEAD : (h + 1) * HEAD], upper)
            SL[n, :128] = full[:128, :128]
            SL[n, 128:] = full[:, 128:]
            return 0

        lax.fori_loop(0, GROUP, one, 0, unroll=4)

    def first_slice(s):
        return W.at[:, y, s, x, c]

    def second_slice(h, s):
        return W.at[h, y, 0, :, c] if s == 0 else W.at[h, :, 1, x, c]

    def core_slice(h):
        return W.at[h, :, :, :, c]

    for s in range(2):
        for k in (1, 2, 3):
            piece = first_slice(s)
            send(piece, piece, s1s.at[s, k - 1], s1r.at[s, k - 1], (at_x, at_y)[s](k))
    for copy in copies[3:]:
        copy.wait()
    slopes(0)
    slopes(1)
    for s in range(2):
        for k in (1, 2, 3):
            wait(first_slice(s), s1r.at[s, k - 1])
    for h in range(HEADS):
        for k in (1, 2, 3):
            for s in range(2):
                piece = second_slice(h, s)
                send(piece, piece, s2s.at[h, s, k - 1], s2r.at[h, s, k - 1], (at_y, at_x)[s](k))
    slopes(2)
    slopes(3)

    def to_core(h):
        for s in range(2):
            for k in (1, 2, 3):
                wait(second_slice(h, s), s2r.at[h, s, k - 1])
        send(core_slice(h), core_slice(h), cs.at[h], cr.at[h], other_core)

    def r0(h):
        send(other.at[h], RC.at[h], rcs.at[h], rcr.at[h], other_core)

    def r1(h):
        wait(RC.at[h], rcr.at[h])

        def add(i, _):
            A[h, i] = (own[h, i] + RC[h, i].astype(F32)).astype(BF)
            return 0

        lax.fori_loop(0, 4, add, 0)
        for k in (1, 2, 3):
            for s in range(2):
                piece = A.at[h, lax.rem(y + k, 4), 0] if s == 0 else A.at[h, :, 1, lax.rem(x + k, 4)]
                send(piece, RA.at[h, s, k - 1], ras.at[h, s, k - 1], rar.at[h, s, k - 1], (at_y, at_x)[s](k))

    def r2(h):
        for s in range(2):
            for k in range(3):
                wait(RA.at[h, s, k], rar.at[h, s, k])
            total = (A[h, y, 0] if s == 0 else A[h, :, 1, x]).astype(F32)
            for k in range(3):
                total = total + RA[h, s, k].astype(F32)
            B[h, s] = total
            for k in (1, 2, 3):
                piece = B.at[h, s, lax.rem((x, y)[s] + k, 4)]
                send(piece, RB.at[h, s, k - 1], rbs.at[h, s, k - 1], rbr.at[h, s, k - 1], (at_x, at_y)[s](k))

    def r3(h):
        for s in range(2):
            for k in range(3):
                wait(RB.at[h, s, k], rbr.at[h, s, k])
            total = B[h, s, (x, y)[s]]
            for k in range(3):
                total = total + RB[h, s, k]
            C[h, s] = total.reshape(4, 16, HEAD)
        for k in range(1, 8):
            there = lax.rem(z + k, 8)
            send(C.at[h, there // 4, lax.rem(there, 4)], RZ.at[h, k - 1], rzs.at[h, k - 1], rzr.at[h, k - 1], at_z(k))

    def r4(h):
        for k in range(1, 8):
            wait(RZ.at[h, k - 1], rzr.at[h, k - 1])
        total = C[h, zh, zl]
        for k in range(7):
            total = total + RZ[h, k]
        gw_out[:, h * HEAD : (h + 1) * HEAD] = total

    def project(h):
        wait(core_slice(h), cr.at[h])
        total = jnp.zeros((TOK, HEAD), F32)
        for i in range(4):
            total = total + dot(tok[:, i * 1024 : (i + 1) * 1024], W[h, i].reshape(1024, HEAD))
        keys[...] = (total * cosine[...] + pltpu.roll(total, half, 1) * sine[...]).astype(BF)

    def attend(h):
        acc[...] = jnp.zeros_like(acc)

        def one(g, _):
            lanes = pl.ds(pl.multiple_of((h * GROUP + g) * HEAD, HEAD), HEAD)
            queries = q[:, lanes]
            scores = dot_nt(keys[...], queries)
            parts = []
            for b in range(2):
                n = (b + 1) * 128
                span = slice(b * 128, (b + 1) * 128)
                s = scores[:n, span] + bias[:n, span]
                top = jnp.max(s, axis=0, keepdims=True)
                expo = jnp.exp2((s - top) * (SCALE * math.log2(math.e)))
                sl = SL[h * GROUP + g, b * 128 : b * 128 + n]
                norm = 1.0 / jnp.sum(expo, axis=0, keepdims=True)
                inner = jnp.sum(expo * sl, axis=0, keepdims=True) * norm
                parts.append((expo * (sl - inner) * (norm * SCALE)).astype(BF))
            low = jnp.concatenate([parts[0], jnp.zeros((128, 128), BF)], axis=0)
            dscores = jnp.concatenate([low, parts[1]], axis=1)
            acc[...] += dot(dscores, queries)
            return 0

        lax.fori_loop(0, GROUP, one, 0, unroll=4)

    def weight(h):
        total = acc[...]
        mine = (total * cosine[...] - pltpu.roll(total, half, 1) * sine[...]).astype(BF)
        gk[:, h * HEAD : (h + 1) * HEAD] = mine

        def give(i, _):
            eight = pl.ds(pl.multiple_of(i * 8, 8), 8)
            given = dot(TT[1, eight].reshape(512, TOK), mine)
            other[h, i] = given.astype(BF).reshape(2, 4, 64, HEAD)
            return 0

        lax.fori_loop(0, 4, give, 0, unroll=4)
        r0(h)

        def keep(i, _):
            eight = pl.ds(pl.multiple_of(i * 8, 8), 8)
            own[h, i] = dot(TT[0, eight].reshape(512, TOK), mine).reshape(2, 4, 64, HEAD)
            return 0

        lax.fori_loop(0, 4, keep, 0, unroll=4)

    def tokens_part(i):
        def one(n, _):
            rows = [W[h, n // 2, n % 2].reshape(512, HEAD) for h in range(HEADS)]
            cols = pl.ds(pl.multiple_of(n * 512, 512), 512)
            gt[:, cols] = dot_nt(gk[...], jnp.concatenate(rows, axis=1)).astype(BF)
            return 0

        lax.fori_loop(2 * i, 2 * i + 2, one, 0)

    to_core(0)
    to_core(1)
    for h in range(HEADS):
        project(h)
        if h + 2 < HEADS:
            to_core(h + 2)
        attend(h)
        if h >= 1:
            r1(h - 1)
        weight(h)
        if h >= 2:
            r2(h - 2)
        if h >= 3:
            r3(h - 3)
    tokens_part(0)
    r1(3)
    r2(2)
    r3(1)
    tokens_part(1)
    tokens_part(2)
    r2(3)
    r3(2)
    r4(0)
    r4(1)
    tokens_part(3)
    r3(3)
    r4(2)
    r4(3)

    for s in range(2):
        for k in range(3):
            wait(first_slice(s), s1s.at[s, k])
    for k in range(7):
        wait(mine, zs.at[k])
    for h in range(HEADS):
        for k in range(3):
            for s in range(2):
                wait(second_slice(h, s), s2s.at[h, s, k])
                wait(RA.at[h, s, k], ras.at[h, s, k])
                wait(RB.at[h, s, k], rbs.at[h, s, k])
        wait(core_slice(h), cs.at[h])
        wait(RC.at[h], rcs.at[h])
        for k in range(7):
            wait(RZ.at[h, k], rzs.at[h, k])


def per_device(tokens, queries, values, upstream, key_weight, positions):
    inputs = (tokens, queries, values, upstream, key_weight, positions.reshape(1, TOK))
    far = pl.BlockSpec(memory_space=pltpu.HBM)
    near = pl.BlockSpec(memory_space=pltpu.VMEM)
    dma = pltpu.SemaphoreType.DMA
    vm = pltpu.VMEM
    return pl.pallas_call(
        kernel,
        out_shape=(pltpu.VMEM((TOK, D), BF), pltpu.VMEM((16, HEADS * HEAD), F32)),
        in_specs=[far] * 6,
        out_specs=(near, near),
        scratch_shapes=[
            vm((HEADS * GROUP, 384, HEAD), F32),
            vm((TOK, D), BF), vm((TOK, D), BF), vm((TOK, HEADS * HEAD), BF), vm((TOK, D), BF),
            vm((16, HEADS * HEAD), BF), vm((1, TOK), jnp.int32),
            vm((HEADS, 4, 2, 4, 2, 4, 16, HEAD), BF),
            vm((2, 32, 64, TOK), BF),
            vm((TOK, HEAD), F32), vm((TOK, HEAD), F32), vm((TOK, TOK), F32),
            vm((TOK, HEAD), BF), vm((TOK, HEAD), F32), vm((TOK, HEADS * HEAD), BF),
            vm((HEADS, 4, 2, 4, 64, HEAD), F32),
            vm((HEADS, 4, 2, 4, 64, HEAD), BF),
            vm((HEADS, 4, 2, 4, 64, HEAD), BF),
            vm((HEADS, 4, 2, 4, 64, HEAD), BF),
            vm((HEADS, 2, 3, 4, 64, HEAD), BF),
            vm((HEADS, 2, 4, 64, HEAD), F32),
            vm((HEADS, 2, 3, 64, HEAD), F32),
            vm((HEADS, 2, 4, 16, HEAD), F32),
            vm((HEADS, 7, 16, HEAD), F32),
            dma((6,)),
            dma((7,)), dma((7,)), dma((2, 3)), dma((2, 3)), dma((HEADS, 2, 3)), dma((HEADS, 2, 3)),
            dma((HEADS,)), dma((HEADS,)),
            dma((HEADS,)), dma((HEADS,)),
            dma((HEADS, 2, 3)), dma((HEADS, 2, 3)), dma((HEADS, 2, 3)), dma((HEADS, 2, 3)),
            dma((HEADS, 7)), dma((HEADS, 7)),
        ],
        compiler_params=pltpu.CompilerParams(
            collective_id=0, has_side_effects=True, vmem_limit_bytes=48 << 20
        ),
        cost_estimate=pl.CostEstimate(
            flops=5_000_000_000, bytes_accessed=9_000_000, transcendentals=2_000_000
        ),
        name="key_backward",
    )(*(pltpu.with_memory_space_constraint(a, pltpu.HBM) for a in inputs))


def solution(mesh):
    torus = Mesh(mesh.devices.reshape(4, 2, 4, 2, mesh.shape["local"]), AXES)
    rows = P(AXES, None)
    return jax.shard_map(
        per_device,
        mesh=torus,
        in_specs=(rows, rows, rows, rows, rows, P(AXES)),
        out_specs=(rows, rows),
        check_vma=False,
    )
```

```python
import math

import jax
import jax.numpy as jnp
from jax import lax
from jax.experimental import pallas as pl
from jax.experimental.pallas import tpu as pltpu
from jax.sharding import Mesh
from jax.sharding import PartitionSpec as P

AXES = ("y", "zh", "x", "c", "zl")
MESH = pl.DeviceIdType.MESH
HEADS = 4
GROUP = 8
HEAD = 128
TOK = 256
D = 4096
SCALE = HEAD**-0.5
BF = jnp.bfloat16
F32 = jnp.float32
NT = (((1,), (1,)), ((), ()))


def dot_nt(a, b):
    return lax.dot_general(a, b, NT, preferred_element_type=F32)


def dot(a, b):
    return jnp.dot(a, b, preferred_element_type=F32)


def kernel(
    tok_hbm, q_hbm, v_hbm, u_hbm, kw_hbm, pos_hbm,
    gt, gw_out,
    SL, tok, q, v, u, kw, pos, W, TT, cosine, sine, bias, keys, acc, gk,
    own, other, RC, A, RA, B, RB, C, RZ,
    load_sem,
    zs, zr, s1s, s1r, s2s, s2r, cs, cr,
    rcs, rcr, ras, rar, rbs, rbr, rzs, rzr,
):
    y, zh, x, c, zl = (lax.axis_index(a) for a in AXES)
    z = zh * 4 + zl
    other_core = (y, zh, x, 1 - c, zl)

    def at_x(k):
        return (y, zh, lax.rem(x + k, 4), c, zl)

    def at_y(k):
        return (lax.rem(y + k, 4), zh, x, c, zl)

    def at_z(k):
        there = lax.rem(z + k, 8)
        return (y, there // 4, x, c, lax.rem(there, 4))

    def send(src, dst, send_sem, recv_sem, where):
        pltpu.make_async_remote_copy(
            src_ref=src, dst_ref=dst, send_sem=send_sem, recv_sem=recv_sem,
            device_id=where, device_id_type=MESH,
        ).start()

    def wait(like, sem):
        pltpu.make_async_copy(like, like, sem).wait()

    loads = [(kw_hbm, kw), (pos_hbm, pos), (tok_hbm, tok), (v_hbm, v), (q_hbm, q), (u_hbm, u)]
    copies = [pltpu.make_async_copy(a, b, load_sem.at[i]) for i, (a, b) in enumerate(loads)]
    for copy in copies:
        copy.start()
    barrier = pltpu.get_barrier_semaphore()
    peers = [other_core] + [at_x(k) for k in (1, 2, 3)] + [at_y(k) for k in (1, 2, 3)]
    peers += [at_z(k) for k in range(1, 8)]
    for peer in peers:
        pl.semaphore_signal(barrier, inc=1, device_id=peer, device_id_type=MESH)
    copies[0].wait()
    for h in range(HEADS):
        W[h, y, zh, x, c, zl] = kw[:, h * HEAD : (h + 1) * HEAD]
    pl.semaphore_wait(barrier, len(peers))

    spans = (slice(0, 1), slice(1, HEADS))
    mine = [W.at[span, y, zh, x, c, zl] for span in spans]
    for p in range(2):
        for k in range(1, 8):
            send(mine[p], mine[p], zs.at[p, k - 1], zr.at[p, k - 1], at_z(k))

    copies[1].wait()
    lane = lax.broadcasted_iota(jnp.int32, (1, HEAD), 1)
    half = HEAD // 2
    freq = jnp.exp(-(lax.rem(lane, half).astype(F32) * 2.0 / HEAD) * math.log(1000000.0))
    place = pos[...].astype(F32)
    column = jnp.broadcast_to(place, (HEAD, TOK)).T
    angle = column * freq
    cosine[...] = jnp.cos(angle)
    sine[...] = jnp.where(lane < half, -1.0, 1.0) * jnp.sin(angle)
    row = lax.broadcasted_iota(jnp.int32, (TOK, TOK), 0)
    col = lax.broadcasted_iota(jnp.int32, (TOK, TOK), 1)
    allowed = (row <= col) & (row >= col - pos[...])
    bias[...] = jnp.where(allowed, 0.0, -1e30).astype(F32)

    copies[2].wait()

    def turn(i, _):
        block = tok[:, pl.ds(pl.multiple_of(i * HEAD, HEAD), HEAD)].T
        TT[c, i] = block[:64]
        TT[1 - c, i] = block[64:]
        return 0

    lax.fori_loop(0, 32, turn, 0)

    def slopes(h):
        def one(g, _):
            n = h * GROUP + g
            upper = u[:, pl.ds(pl.multiple_of(n * HEAD, HEAD), HEAD)]
            full = dot_nt(v[:, h * HEAD : (h + 1) * HEAD], upper)
            SL[n, :128] = full[:128, :128]
            SL[n, 128:] = full[:, 128:]
            return 0

        lax.fori_loop(0, GROUP, one, 0, unroll=4)

    def first_slice(p, s):
        return W.at[spans[p], y, s, x, c]

    def second_slice(h, s):
        return W.at[h, y, 0, :, c] if s == 0 else W.at[h, :, 1, x, c]

    def core_slice(h):
        return W.at[h, :, :, :, c]

    three = pl.ds(0, 3)

    def first_slots(p, s):
        return W.at[spans[p], y, s, three, c]

    def second_slots(h, s):
        return W.at[h, three, 0, :, c] if s == 0 else W.at[h, :, 1, three, c]

    def first_stage(p):
        for k in range(7):
            wait(mine[p], zr.at[p, k])
        for k in (1, 2, 3):
            for s in range(2):
                piece = first_slice(p, s)
                send(piece, piece, s1s.at[p, s], s1r.at[p, s], (at_x, at_y)[s](k))

    def second_stage(p):
        for s in range(2):
            wait(first_slots(p, s), s1r.at[p, s])
        for h in range(HEADS)[spans[p]]:
            for k in (1, 2, 3):
                for s in range(2):
                    piece = second_slice(h, s)
                    send(piece, piece, s2s.at[h, s], s2r.at[h, s], (at_y, at_x)[s](k))

    first_stage(0)
    first_stage(1)
    for copy in copies[3:]:
        copy.wait()
    slopes(0)
    second_stage(0)
    second_stage(1)
    slopes(1)
    slopes(2)

    def to_core(h):
        for s in range(2):
            wait(second_slots(h, s), s2r.at[h, s])
        send(core_slice(h), core_slice(h), cs.at[h], cr.at[h], other_core)

    def r0(h):
        send(other.at[h], RC.at[h], rcs.at[h], rcr.at[h], other_core)

    def r1(h):
        wait(RC.at[h], rcr.at[h])

        def add(i, _):
            A[h, i] = (own[h, i] + RC[h, i].astype(F32)).astype(BF)
            return 0

        lax.fori_loop(0, 4, add, 0)
        for k in (1, 2, 3):
            for s in range(2):
                piece = A.at[h, lax.rem(y + k, 4), 0] if s == 0 else A.at[h, :, 1, lax.rem(x + k, 4)]
                send(piece, RA.at[h, s, k - 1], ras.at[h, s], rar.at[h, s], (at_y, at_x)[s](k))

    def r2(h):
        for s in range(2):
            wait(RA.at[h, s], rar.at[h, s])
            total = (A[h, y, 0] if s == 0 else A[h, :, 1, x]).astype(F32)
            for k in range(3):
                total = total + RA[h, s, k].astype(F32)
            B[h, s] = total

    sets = (slice(0, 2), slice(2, 3), slice(3, 4))

    def to_second(n):
        for k in (1, 2, 3):
            for s in range(2):
                piece = B.at[sets[n], s, lax.rem((x, y)[s] + k, 4)]
                send(piece, RB.at[sets[n], s, k - 1], rbs.at[n, s], rbr.at[n, s], (at_x, at_y)[s](k))

    def r3(n):
        for s in range(2):
            wait(RB.at[sets[n], s], rbr.at[n, s])
            for h in range(HEADS)[sets[n]]:
                total = B[h, s, (x, y)[s]]
                for k in range(3):
                    total = total + RB[h, s, k]
                C[h, s] = total.reshape(4, 16, HEAD)
        for k in range(1, 8):
            there = lax.rem(z + k, 8)
            piece = C.at[sets[n], there // 4, lax.rem(there, 4)]
            send(piece, RZ.at[sets[n], k - 1], rzs.at[n], rzr.at[n], at_z(k))

    def r4(n):
        wait(RZ.at[sets[n]], rzr.at[n])
        for h in range(HEADS)[sets[n]]:
            total = C[h, zh, zl]
            for k in range(7):
                total = total + RZ[h, k]
            gw_out[:, h * HEAD : (h + 1) * HEAD] = total

    def project(h):
        wait(core_slice(h), cr.at[h])
        total = jnp.zeros((TOK, HEAD), F32)
        for i in range(4):
            total = total + dot(tok[:, i * 1024 : (i + 1) * 1024], W[h, i].reshape(1024, HEAD))
        keys[...] = (total * cosine[...] + pltpu.roll(total, half, 1) * sine[...]).astype(BF)

    def attend(h):
        acc[...] = jnp.zeros_like(acc)

        def one(g, _):
            lanes = pl.ds(pl.multiple_of((h * GROUP + g) * HEAD, HEAD), HEAD)
            queries = q[:, lanes]
            scores = dot_nt(keys[...], queries)
            parts = []
            for b in range(2):
                n = (b + 1) * 128
                span = slice(b * 128, (b + 1) * 128)
                s = scores[:n, span] + bias[:n, span]
                top = jnp.max(s, axis=0, keepdims=True)
                expo = jnp.exp2((s - top) * (SCALE * math.log2(math.e)))
                sl = SL[h * GROUP + g, b * 128 : b * 128 + n]
                norm = 1.0 / jnp.sum(expo, axis=0, keepdims=True)
                inner = jnp.sum(expo * sl, axis=0, keepdims=True) * norm
                parts.append((expo * (sl - inner) * (norm * SCALE)).astype(BF))
            low = jnp.concatenate([parts[0], jnp.zeros((128, 128), BF)], axis=0)
            dscores = jnp.concatenate([low, parts[1]], axis=1)
            acc[...] += dot(dscores, queries)
            return 0

        lax.fori_loop(0, GROUP, one, 0, unroll=8)

    def weight(h):
        total = acc[...]
        mine = (total * cosine[...] - pltpu.roll(total, half, 1) * sine[...]).astype(BF)
        gk[:, h * HEAD : (h + 1) * HEAD] = mine

        def give(i, _):
            eight = pl.ds(pl.multiple_of(i * 8, 8), 8)
            given = dot(TT[1, eight].reshape(512, TOK), mine)
            other[h, i] = given.astype(BF).reshape(2, 4, 64, HEAD)
            return 0

        lax.fori_loop(0, 4, give, 0, unroll=4)
        r0(h)

        def keep(i, _):
            eight = pl.ds(pl.multiple_of(i * 8, 8), 8)
            own[h, i] = dot(TT[0, eight].reshape(512, TOK), mine).reshape(2, 4, 64, HEAD)
            return 0

        lax.fori_loop(0, 4, keep, 0, unroll=4)

    def tokens_part(i, j):
        def one(n, _):
            rows = [W[h, n // 2, n % 2].reshape(512, HEAD) for h in range(HEADS)]
            cols = pl.ds(pl.multiple_of(n * 512, 512), 512)
            gt[:, cols] = dot_nt(gk[...], jnp.concatenate(rows, axis=1)).astype(BF)
            return 0

        lax.fori_loop(i, j, one, 0)

    to_core(0)
    slopes(3)
    for h in range(HEADS):
        project(h)
        if h == 0:
            to_core(1)
            to_core(2)
        elif h == 1:
            to_core(3)
        attend(h)
        if h >= 1:
            r1(h - 1)
        if h >= 3:
            r2(h - 3)
        weight(h)

    def gather_sent():
        for p in range(2):
            for k in range(7):
                wait(mine[p], zs.at[p, k])
            for s in range(2):
                wait(first_slots(p, s), s1s.at[p, s])
        for h in range(HEADS):
            for s in range(2):
                wait(second_slots(h, s), s2s.at[h, s])
            wait(core_slice(h), cs.at[h])

    r2(1)
    to_second(0)
    tokens_part(0, 2)
    r1(3)
    tokens_part(2, 5)
    r2(2)
    to_second(1)
    r3(0)
    tokens_part(5, 7)
    r2(3)
    to_second(2)
    tokens_part(7, 8)
    gather_sent()
    r3(1)
    r3(2)
    for h in range(HEADS):
        wait(RC.at[h], rcs.at[h])
        for s in range(2):
            wait(RA.at[h, s], ras.at[h, s])
    for n in range(3):
        for s in range(2):
            wait(RB.at[sets[n], s], rbs.at[n, s])
    r4(0)
    r4(1)
    r4(2)
    for n in range(3):
        wait(RZ.at[sets[n]], rzs.at[n])


def per_device(tokens, queries, values, upstream, key_weight, positions):
    inputs = (tokens, queries, values, upstream, key_weight, positions.reshape(1, TOK))
    far = pl.BlockSpec(memory_space=pltpu.HBM)
    near = pl.BlockSpec(memory_space=pltpu.VMEM)
    dma = pltpu.SemaphoreType.DMA
    vm = pltpu.VMEM
    return pl.pallas_call(
        kernel,
        out_shape=(pltpu.VMEM((TOK, D), BF), pltpu.VMEM((16, HEADS * HEAD), F32)),
        in_specs=[far] * 6,
        out_specs=(near, near),
        scratch_shapes=[
            vm((HEADS * GROUP, 384, HEAD), F32),
            vm((TOK, D), BF), vm((TOK, D), BF), vm((TOK, HEADS * HEAD), BF), vm((TOK, D), BF),
            vm((16, HEADS * HEAD), BF), vm((1, TOK), jnp.int32),
            vm((HEADS, 4, 2, 4, 2, 4, 16, HEAD), BF),
            vm((2, 32, 64, TOK), BF),
            vm((TOK, HEAD), F32), vm((TOK, HEAD), F32), vm((TOK, TOK), F32),
            vm((TOK, HEAD), BF), vm((TOK, HEAD), F32), vm((TOK, HEADS * HEAD), BF),
            vm((HEADS, 4, 2, 4, 64, HEAD), F32),
            vm((HEADS, 4, 2, 4, 64, HEAD), BF),
            vm((HEADS, 4, 2, 4, 64, HEAD), BF),
            vm((HEADS, 4, 2, 4, 64, HEAD), BF),
            vm((HEADS, 2, 3, 4, 64, HEAD), BF),
            vm((HEADS, 2, 4, 64, HEAD), F32),
            vm((HEADS, 2, 3, 64, HEAD), F32),
            vm((HEADS, 2, 4, 16, HEAD), F32),
            vm((HEADS, 7, 16, HEAD), F32),
            dma((6,)),
            dma((2, 7)), dma((2, 7)), dma((2, 2)), dma((2, 2)), dma((HEADS, 2)), dma((HEADS, 2)),
            dma((HEADS,)), dma((HEADS,)),
            dma((HEADS,)), dma((HEADS,)),
            dma((HEADS, 2)), dma((HEADS, 2)), dma((3, 2)), dma((3, 2)),
            dma((3,)), dma((3,)),
        ],
        compiler_params=pltpu.CompilerParams(
            collective_id=0, has_side_effects=True, vmem_limit_bytes=48 << 20
        ),
        cost_estimate=pl.CostEstimate(
            flops=5_000_000_000, bytes_accessed=9_000_000, transcendentals=2_000_000
        ),
        name="key_backward",
    )(*(pltpu.with_memory_space_constraint(a, pltpu.HBM) for a in inputs))


def solution(mesh):
    torus = Mesh(mesh.devices.reshape(4, 2, 4, 2, mesh.shape["local"]), AXES)
    rows = P(AXES, None)
    return jax.shard_map(
        per_device,
        mesh=torus,
        in_specs=(rows, rows, rows, rows, rows, P(AXES)),
        out_specs=(rows, rows),
        check_vma=False,
    )
```

```python
import math

import jax
import jax.numpy as jnp
from jax import lax
from jax.experimental import pallas as pl
from jax.experimental.pallas import tpu as pltpu
from jax.sharding import Mesh
from jax.sharding import PartitionSpec as P

AXES = ("y", "zh", "x", "c", "zl")
MESH = pl.DeviceIdType.MESH
HEADS = 4
GROUP = 8
HEAD = 128
TOK = 256
D = 4096
SCALE = HEAD**-0.5
BF = jnp.bfloat16
F32 = jnp.float32
FAR4 = (2, 1, 3)
FAR8 = (4, 3, 5, 2, 6, 1, 7)
NT = (((1,), (1,)), ((), ()))


def dot_nt(a, b):
    return lax.dot_general(a, b, NT, preferred_element_type=F32)


def dot(a, b):
    return jnp.dot(a, b, preferred_element_type=F32)


def kernel(
    tok_hbm, q_hbm, v_hbm, u_hbm, kw_hbm, pos_hbm,
    gt, gw_out,
    SL, tok, q, v, u, kw, pos, W, TT, cosine, sine, bias, keys, acc, gk,
    own, other, RC, A, RA, B, RB, C, RZ,
    load_sem,
    zs, zr, s1s, s1r, s2s, s2r, cs, cr,
    rcs, rcr, ras, rar, rbs, rbr, rzs, rzr,
):
    y, zh, x, c, zl = (lax.axis_index(a) for a in AXES)
    z = zh * 4 + zl
    other_core = (y, zh, x, 1 - c, zl)

    def at_x(k):
        return (y, zh, lax.rem(x + k, 4), c, zl)

    def at_y(k):
        return (lax.rem(y + k, 4), zh, x, c, zl)

    def at_z(k):
        there = lax.rem(z + k, 8)
        return (y, there // 4, x, c, lax.rem(there, 4))

    def send(src, dst, send_sem, recv_sem, where):
        pltpu.make_async_remote_copy(
            src_ref=src, dst_ref=dst, send_sem=send_sem, recv_sem=recv_sem,
            device_id=where, device_id_type=MESH,
        ).start()

    def wait(like, sem):
        pltpu.make_async_copy(like, like, sem).wait()

    barrier = pltpu.get_barrier_semaphore()
    peers = [at_z(k) for k in FAR8] + [f(k) for k in FAR4 for f in (at_x, at_y)] + [other_core]
    for peer in peers:
        pl.semaphore_signal(barrier, inc=1, device_id=peer, device_id_type=MESH)
    loads = [(kw_hbm, kw), (pos_hbm, pos), (tok_hbm, tok), (v_hbm, v), (q_hbm, q), (u_hbm, u)]
    copies = [pltpu.make_async_copy(a, b, load_sem.at[i]) for i, (a, b) in enumerate(loads)]
    for copy in copies:
        copy.start()
    copies[0].wait()
    for h in range(HEADS):
        W[h, y, zh, x, c, zl] = kw[:, h * HEAD : (h + 1) * HEAD]
    pl.semaphore_wait(barrier, len(peers))

    spans = (slice(0, 1), slice(1, HEADS))
    mine = [W.at[span, y, zh, x, c, zl] for span in spans]
    for p in range(2):
        for k in FAR8:
            send(mine[p], mine[p], zs.at[p, k - 1], zr.at[p, k - 1], at_z(k))

    copies[1].wait()
    lane = lax.broadcasted_iota(jnp.int32, (1, HEAD), 1)
    half = HEAD // 2
    freq = jnp.exp(-(lax.rem(lane, half).astype(F32) * 2.0 / HEAD) * math.log(1000000.0))
    place = pos[...].astype(F32)
    column = jnp.broadcast_to(place, (HEAD, TOK)).T
    angle = column * freq
    cosine[...] = jnp.cos(angle)
    sine[...] = jnp.where(lane < half, -1.0, 1.0) * jnp.sin(angle)
    row = lax.broadcasted_iota(jnp.int32, (TOK, TOK), 0)
    col = lax.broadcasted_iota(jnp.int32, (TOK, TOK), 1)
    allowed = (row <= col) & (row >= col - pos[...])
    bias[...] = jnp.where(allowed, 0.0, -1e30).astype(F32)

    copies[2].wait()

    def turn(i, _):
        block = tok[:, pl.ds(pl.multiple_of(i * HEAD, HEAD), HEAD)].T
        TT[c, i] = block[:64]
        TT[1 - c, i] = block[64:]
        return 0

    lax.fori_loop(0, 32, turn, 0)

    def slopes(h):
        def one(g, _):
            n = h * GROUP + g
            upper = u[:, pl.ds(pl.multiple_of(n * HEAD, HEAD), HEAD)]
            full = dot_nt(v[:, h * HEAD : (h + 1) * HEAD], upper)
            SL[n, :128] = full[:128, :128]
            SL[n, 128:] = full[:, 128:]
            return 0

        lax.fori_loop(0, GROUP, one, 0, unroll=4)

    def first_slice(p, s):
        return W.at[spans[p], y, s, x, c]

    def second_slice(h, s):
        return W.at[h, y, 0, :, c] if s == 0 else W.at[h, :, 1, x, c]

    def core_slice(h):
        return W.at[h, :, :, :, c]

    three = pl.ds(0, 3)

    def first_slots(p, s):
        return W.at[spans[p], y, s, three, c]

    def second_slots(h, s):
        return W.at[h, three, 0, :, c] if s == 0 else W.at[h, :, 1, three, c]

    def first_stage(p):
        for k in range(7):
            wait(mine[p], zr.at[p, k])
        for k in FAR4:
            for s in range(2):
                piece = first_slice(p, s)
                send(piece, piece, s1s.at[p, s], s1r.at[p, s], (at_x, at_y)[s](k))

    def second_stage(p):
        for s in range(2):
            wait(first_slots(p, s), s1r.at[p, s])
        for h in range(HEADS)[spans[p]]:
            for k in FAR4:
                for s in range(2):
                    piece = second_slice(h, s)
                    send(piece, piece, s2s.at[h, s], s2r.at[h, s], (at_y, at_x)[s](k))

    first_stage(0)
    first_stage(1)
    for copy in copies[3:]:
        copy.wait()
    slopes(0)
    second_stage(0)
    second_stage(1)
    slopes(1)
    slopes(2)

    def to_core(h):
        for s in range(2):
            wait(second_slots(h, s), s2r.at[h, s])
        send(core_slice(h), core_slice(h), cs.at[h], cr.at[h], other_core)

    def r0(h):
        send(other.at[h], RC.at[h], rcs.at[h], rcr.at[h], other_core)

    def r1(h):
        wait(RC.at[h], rcr.at[h])

        def add(i, _):
            A[h, i] = (own[h, i] + RC[h, i].astype(F32)).astype(BF)
            return 0

        lax.fori_loop(0, 4, add, 0)
        for k in FAR4:
            for s in range(2):
                piece = A.at[h, lax.rem(y + k, 4), 0] if s == 0 else A.at[h, :, 1, lax.rem(x + k, 4)]
                send(piece, RA.at[h, s, k - 1], ras.at[h, s], rar.at[h, s], (at_y, at_x)[s](k))

    def r2(h):
        for s in range(2):
            wait(RA.at[h, s], rar.at[h, s])
            total = (A[h, y, 0] if s == 0 else A[h, :, 1, x]).astype(F32)
            for k in range(3):
                total = total + RA[h, s, k].astype(F32)
            B[h, s] = total

    sets = (slice(0, 2), slice(2, 3), slice(3, 4))

    def to_second(n):
        for k in FAR4:
            for s in range(2):
                piece = B.at[sets[n], s, lax.rem((x, y)[s] + k, 4)]
                send(piece, RB.at[sets[n], s, k - 1], rbs.at[n, s], rbr.at[n, s], (at_x, at_y)[s](k))

    def r3(n):
        for s in range(2):
            wait(RB.at[sets[n], s], rbr.at[n, s])
            for h in range(HEADS)[sets[n]]:
                total = B[h, s, (x, y)[s]]
                for k in range(3):
                    total = total + RB[h, s, k]
                C[h, s] = total.reshape(4, 16, HEAD)
        for k in FAR8:
            there = lax.rem(z + k, 8)
            piece = C.at[sets[n], there // 4, lax.rem(there, 4)]
            send(piece, RZ.at[sets[n], k - 1], rzs.at[n], rzr.at[n], at_z(k))

    def r4(n):
        wait(RZ.at[sets[n]], rzr.at[n])
        for h in range(HEADS)[sets[n]]:
            total = C[h, zh, zl]
            for k in range(7):
                total = total + RZ[h, k]
            gw_out[:, h * HEAD : (h + 1) * HEAD] = total

    def project(*heads):
        for h in heads:
            wait(core_slice(h), cr.at[h])
        total = jnp.zeros((TOK, len(heads) * HEAD), F32)
        for i in range(4):
            rows = jnp.concatenate([W[h, i].reshape(1024, HEAD) for h in heads], axis=1)
            total = total + dot(tok[:, i * 1024 : (i + 1) * 1024], rows)
        for i, h in enumerate(heads):
            raw = total[:, i * HEAD : (i + 1) * HEAD]
            keys[h] = (raw * cosine[...] + pltpu.roll(raw, half, 1) * sine[...]).astype(BF)

    def attend(h):
        acc[...] = jnp.zeros_like(acc)

        def one(g, _):
            lanes = pl.ds(pl.multiple_of((h * GROUP + g) * HEAD, HEAD), HEAD)
            queries = q[:, lanes]
            scores = dot_nt(keys[h], queries)
            parts = []
            for b in range(2):
                n = (b + 1) * 128
                span = slice(b * 128, (b + 1) * 128)
                s = scores[:n, span] + bias[:n, span]
                top = jnp.max(s, axis=0, keepdims=True)
                expo = jnp.exp2((s - top) * (SCALE * math.log2(math.e)))
                sl = SL[h * GROUP + g, b * 128 : b * 128 + n]
                norm = 1.0 / jnp.sum(expo, axis=0, keepdims=True)
                inner = jnp.sum(expo * sl, axis=0, keepdims=True) * norm
                parts.append((expo * (sl - inner) * (norm * SCALE)).astype(BF))
            low = jnp.concatenate([parts[0], jnp.zeros((128, 128), BF)], axis=0)
            dscores = jnp.concatenate([low, parts[1]], axis=1)
            acc[...] += dot(dscores, queries)
            return 0

        lax.fori_loop(0, GROUP, one, 0, unroll=8)

    def weight(h):
        total = acc[...]
        mine = (total * cosine[...] - pltpu.roll(total, half, 1) * sine[...]).astype(BF)
        gk[:, h * HEAD : (h + 1) * HEAD] = mine

        def give(i, _):
            eight = pl.ds(pl.multiple_of(i * 8, 8), 8)
            given = dot(TT[1, eight].reshape(512, TOK), mine)
            other[h, i] = given.astype(BF).reshape(2, 4, 64, HEAD)
            return 0

        lax.fori_loop(0, 4, give, 0, unroll=4)
        r0(h)

        def keep(i, _):
            eight = pl.ds(pl.multiple_of(i * 8, 8), 8)
            own[h, i] = dot(TT[0, eight].reshape(512, TOK), mine).reshape(2, 4, 64, HEAD)
            return 0

        lax.fori_loop(0, 4, keep, 0, unroll=4)

    def tokens_part(i, j):
        def one(n, _):
            rows = [W[h, n // 2, n % 2].reshape(512, HEAD) for h in range(HEADS)]
            cols = pl.ds(pl.multiple_of(n * 512, 512), 512)
            gt[:, cols] = dot_nt(gk[...], jnp.concatenate(rows, axis=1)).astype(BF)
            return 0

        lax.fori_loop(i, j, one, 0)

    to_core(0)
    slopes(3)
    for h in range(HEADS):
        if h < 2:
            project(h)
        elif h == 2:
            project(2, 3)
        if h == 0:
            to_core(1)
            to_core(2)
        elif h == 1:
            to_core(3)
        attend(h)
        if h >= 1:
            r1(h - 1)
        if h >= 3:
            r2(h - 3)
        weight(h)

    def gather_sent():
        for p in range(2):
            for k in range(7):
                wait(mine[p], zs.at[p, k])
            for s in range(2):
                wait(first_slots(p, s), s1s.at[p, s])
        for h in range(HEADS):
            for s in range(2):
                wait(second_slots(h, s), s2s.at[h, s])
            wait(core_slice(h), cs.at[h])

    r2(1)
    to_second(0)
    tokens_part(0, 2)
    r1(3)
    tokens_part(2, 5)
    r2(2)
    to_second(1)
    r3(0)
    tokens_part(5, 7)
    r2(3)
    to_second(2)
    tokens_part(7, 8)
    gather_sent()
    r3(1)
    r3(2)
    for h in range(HEADS):
        wait(RC.at[h], rcs.at[h])
        for s in range(2):
            wait(RA.at[h, s], ras.at[h, s])
    for n in range(3):
        for s in range(2):
            wait(RB.at[sets[n], s], rbs.at[n, s])
    r4(0)
    r4(1)
    r4(2)
    for n in range(3):
        wait(RZ.at[sets[n]], rzs.at[n])


def hand_over(gt, gw, gt_hbm, gw_hbm, sem):
    copies = [pltpu.make_async_copy(a, b, sem.at[i]) for i, (a, b) in enumerate(((gw, gw_hbm), (gt, gt_hbm)))]
    for copy in copies:
        copy.start()
    for copy in copies:
        copy.wait()


def per_device(tokens, queries, values, upstream, key_weight, positions):
    inputs = (tokens, queries, values, upstream, key_weight, positions.reshape(1, TOK))
    far = pl.BlockSpec(memory_space=pltpu.HBM)
    near = pl.BlockSpec(memory_space=pltpu.VMEM)
    dma = pltpu.SemaphoreType.DMA
    vm = pltpu.VMEM
    results = pl.pallas_call(
        kernel,
        out_shape=(pltpu.VMEM((TOK, D), BF), pltpu.VMEM((16, HEADS * HEAD), F32)),
        in_specs=[far] * 6,
        out_specs=(near, near),
        scratch_shapes=[
            vm((HEADS * GROUP, 384, HEAD), F32),
            vm((TOK, D), BF), vm((TOK, D), BF), vm((TOK, HEADS * HEAD), BF), vm((TOK, D), BF),
            vm((16, HEADS * HEAD), BF), vm((1, TOK), jnp.int32),
            vm((HEADS, 4, 2, 4, 2, 4, 16, HEAD), BF),
            vm((2, 32, 64, TOK), BF),
            vm((TOK, HEAD), F32), vm((TOK, HEAD), F32), vm((TOK, TOK), F32),
            vm((HEADS, TOK, HEAD), BF), vm((TOK, HEAD), F32), vm((TOK, HEADS * HEAD), BF),
            vm((HEADS, 4, 2, 4, 64, HEAD), F32),
            vm((HEADS, 4, 2, 4, 64, HEAD), BF),
            vm((HEADS, 4, 2, 4, 64, HEAD), BF),
            vm((HEADS, 4, 2, 4, 64, HEAD), BF),
            vm((HEADS, 2, 3, 4, 64, HEAD), BF),
            vm((HEADS, 2, 4, 64, HEAD), F32),
            vm((HEADS, 2, 3, 64, HEAD), F32),
            vm((HEADS, 2, 4, 16, HEAD), F32),
            vm((HEADS, 7, 16, HEAD), F32),
            dma((6,)),
            dma((2, 7)), dma((2, 7)), dma((2, 2)), dma((2, 2)), dma((HEADS, 2)), dma((HEADS, 2)),
            dma((HEADS,)), dma((HEADS,)),
            dma((HEADS,)), dma((HEADS,)),
            dma((HEADS, 2)), dma((HEADS, 2)), dma((3, 2)), dma((3, 2)),
            dma((3,)), dma((3,)),
        ],
        compiler_params=pltpu.CompilerParams(
            collective_id=0, has_side_effects=True, vmem_limit_bytes=48 << 20
        ),
        cost_estimate=pl.CostEstimate(
            flops=5_000_000_000, bytes_accessed=9_000_000, transcendentals=2_000_000
        ),
        name="key_backward",
    )(*(pltpu.with_memory_space_constraint(a, pltpu.HBM) for a in inputs))
    return pl.pallas_call(
        hand_over,
        out_shape=(jax.ShapeDtypeStruct((TOK, D), BF), jax.ShapeDtypeStruct((16, HEADS * HEAD), F32)),
        in_specs=[near] * 2,
        out_specs=(far, far),
        scratch_shapes=[dma((2,))],
        name="hand_over",
    )(*(pltpu.with_memory_space_constraint(a, pltpu.VMEM) for a in results))


def solution(mesh):
    torus = Mesh(mesh.devices.reshape(4, 2, 4, 2, mesh.shape["local"]), AXES)
    rows = P(AXES, None)
    return jax.shard_map(
        per_device,
        mesh=torus,
        in_specs=(rows, rows, rows, rows, rows, P(AXES)),
        out_specs=(rows, rows),
        check_vma=False,
    )
```

```python
import math

import jax
import jax.numpy as jnp
from jax import lax
from jax.experimental import pallas as pl
from jax.experimental.pallas import tpu as pltpu
from jax.sharding import Mesh
from jax.sharding import PartitionSpec as P

AXES = ("y", "zh", "x", "c", "zl")
MESH = pl.DeviceIdType.MESH
HEADS = 4
GROUP = 8
HEAD = 128
TOK = 256
D = 4096
SCALE = HEAD**-0.5
BF = jnp.bfloat16
F32 = jnp.float32
FAR4 = (2, 1, 3)
FAR8 = (4, 3, 5, 2, 6, 1, 7)
NT = (((1,), (1,)), ((), ()))


def dot_nt(a, b):
    return lax.dot_general(a, b, NT, preferred_element_type=F32)


def dot(a, b):
    return jnp.dot(a, b, preferred_element_type=F32)


def kernel(
    tok_hbm, q_hbm, v_hbm, u_hbm, kw_hbm, pos_hbm,
    gt, gw_out,
    SL, tok, q, v, u, kw, pos, W, TT, cosine, sine, bias, keys, acc, gk,
    own, other, RC, A, RA, B, RB, C, RZ,
    load_sem,
    zs, zr, s1s, s1r, s2s, s2r, cs, cr,
    rcs, rcr, ras, rar, rbs, rbr, rzs, rzr,
):
    y, zh, x, c, zl = (lax.axis_index(a) for a in AXES)
    z = zh * 4 + zl
    other_core = (y, zh, x, 1 - c, zl)

    def at_x(k):
        return (y, zh, lax.rem(x + k, 4), c, zl)

    def at_y(k):
        return (lax.rem(y + k, 4), zh, x, c, zl)

    def at_z(k):
        there = lax.rem(z + k, 8)
        return (y, there // 4, x, c, lax.rem(there, 4))

    def send(src, dst, send_sem, recv_sem, where):
        pltpu.make_async_remote_copy(
            src_ref=src, dst_ref=dst, send_sem=send_sem, recv_sem=recv_sem,
            device_id=where, device_id_type=MESH,
        ).start()

    def wait(like, sem):
        pltpu.make_async_copy(like, like, sem).wait()

    barrier = pltpu.get_barrier_semaphore()
    peers = [at_z(k) for k in FAR8] + [f(k) for k in FAR4 for f in (at_x, at_y)] + [other_core]
    for peer in peers:
        pl.semaphore_signal(barrier, inc=1, device_id=peer, device_id_type=MESH)
    loads = [(kw_hbm, kw), (pos_hbm, pos), (tok_hbm, tok), (v_hbm, v), (q_hbm, q), (u_hbm, u)]
    copies = [pltpu.make_async_copy(a, b, load_sem.at[i]) for i, (a, b) in enumerate(loads)]
    for copy in copies:
        copy.start()
    copies[0].wait()
    for h in range(HEADS):
        W[h, y, zh, x, c, zl] = kw[:, h * HEAD : (h + 1) * HEAD]
    pl.semaphore_wait(barrier, len(peers))

    spans = (slice(0, 1), slice(1, HEADS))
    mine = [W.at[span, y, zh, x, c, zl] for span in spans]
    for p in range(2):
        for k in FAR8:
            send(mine[p], mine[p], zs.at[p, k - 1], zr.at[p, k - 1], at_z(k))

    copies[1].wait()
    lane = lax.broadcasted_iota(jnp.int32, (1, HEAD), 1)
    half = HEAD // 2
    freq = jnp.exp(-(lax.rem(lane, half).astype(F32) * 2.0 / HEAD) * math.log(1000000.0))
    place = pos[...].astype(F32)
    column = jnp.broadcast_to(place, (HEAD, TOK)).T
    angle = column * freq
    cosine[...] = jnp.cos(angle)
    sine[...] = jnp.where(lane < half, -1.0, 1.0) * jnp.sin(angle)
    row = lax.broadcasted_iota(jnp.int32, (TOK, TOK), 0)
    col = lax.broadcasted_iota(jnp.int32, (TOK, TOK), 1)
    allowed = (row <= col) & (row >= col - pos[...])
    bias[...] = jnp.where(allowed, 0.0, -1e30).astype(F32)

    copies[2].wait()

    def turn(i, _):
        block = tok[:, pl.ds(pl.multiple_of(i * HEAD, HEAD), HEAD)].T
        TT[c, i] = block[:64]
        TT[1 - c, i] = block[64:]
        return 0

    lax.fori_loop(0, 32, turn, 0)

    def slopes(h):
        def one(g, _):
            n = h * GROUP + g
            upper = u[:, pl.ds(pl.multiple_of(n * HEAD, HEAD), HEAD)]
            full = dot_nt(v[:, h * HEAD : (h + 1) * HEAD], upper)
            SL[n, :128] = full[:128, :128]
            SL[n, 128:] = full[:, 128:]
            return 0

        lax.fori_loop(0, GROUP, one, 0, unroll=4)

    def first_slice(p, s):
        return W.at[spans[p], y, s, x, c]

    def second_slice(h, s):
        return W.at[h, y, 0, :, c] if s == 0 else W.at[h, :, 1, x, c]

    def core_slice(h):
        return W.at[h, :, :, :, c]

    three = pl.ds(0, 3)

    def first_slots(p, s):
        return W.at[spans[p], y, s, three, c]

    def second_slots(h, s):
        return W.at[h, three, 0, :, c] if s == 0 else W.at[h, :, 1, three, c]

    def first_stage(p):
        for k in range(7):
            wait(mine[p], zr.at[p, k])
        for k in FAR4:
            for s in range(2):
                piece = first_slice(p, s)
                send(piece, piece, s1s.at[p, s], s1r.at[p, s], (at_x, at_y)[s](k))

    def second_stage(p):
        for s in range(2):
            wait(first_slots(p, s), s1r.at[p, s])
        for h in range(HEADS)[spans[p]]:
            for k in FAR4:
                for s in range(2):
                    piece = second_slice(h, s)
                    send(piece, piece, s2s.at[h, s], s2r.at[h, s], (at_y, at_x)[s](k))

    first_stage(0)
    first_stage(1)
    for copy in copies[3:]:
        copy.wait()
    slopes(0)
    second_stage(0)
    second_stage(1)
    slopes(1)
    slopes(2)

    def to_core(h):
        for s in range(2):
            wait(second_slots(h, s), s2r.at[h, s])
        send(core_slice(h), core_slice(h), cs.at[h], cr.at[h], other_core)

    def r0(h):
        send(other.at[h], RC.at[h], rcs.at[h], rcr.at[h], other_core)

    def r1(h):
        wait(RC.at[h], rcr.at[h])

        def add(i, _):
            A[h, i] = (own[h, i] + RC[h, i].astype(F32)).astype(BF)
            return 0

        lax.fori_loop(0, 4, add, 0)
        for k in FAR4:
            for s in range(2):
                piece = A.at[h, lax.rem(y + k, 4), 0] if s == 0 else A.at[h, :, 1, lax.rem(x + k, 4)]
                send(piece, RA.at[h, s, k - 1], ras.at[h, s], rar.at[h, s], (at_y, at_x)[s](k))

    def r2(h):
        for s in range(2):
            wait(RA.at[h, s], rar.at[h, s])
            total = (A[h, y, 0] if s == 0 else A[h, :, 1, x]).astype(F32)
            for k in range(3):
                total = total + RA[h, s, k].astype(F32)
            B[h, s] = total

    sets = (slice(0, 2), slice(2, 3), slice(3, 4))

    def to_second(n):
        for k in FAR4:
            for s in range(2):
                piece = B.at[sets[n], s, lax.rem((x, y)[s] + k, 4)]
                send(piece, RB.at[sets[n], s, k - 1], rbs.at[n, s], rbr.at[n, s], (at_x, at_y)[s](k))

    def r3(n):
        for s in range(2):
            wait(RB.at[sets[n], s], rbr.at[n, s])
            for h in range(HEADS)[sets[n]]:
                total = B[h, s, (x, y)[s]]
                for k in range(3):
                    total = total + RB[h, s, k]
                C[h, s] = total.reshape(4, 16, HEAD)
        for k in FAR8:
            there = lax.rem(z + k, 8)
            piece = C.at[sets[n], there // 4, lax.rem(there, 4)]
            send(piece, RZ.at[sets[n], k - 1], rzs.at[n], rzr.at[n], at_z(k))

    def r4(n):
        wait(RZ.at[sets[n]], rzr.at[n])
        for h in range(HEADS)[sets[n]]:
            total = C[h, zh, zl]
            for k in range(7):
                total = total + RZ[h, k]
            gw_out[:, h * HEAD : (h + 1) * HEAD] = total

    def project(*heads):
        for h in heads:
            wait(core_slice(h), cr.at[h])
        total = jnp.zeros((TOK, len(heads) * HEAD), F32)
        for i in range(4):
            rows = jnp.concatenate([W[h, i].reshape(1024, HEAD) for h in heads], axis=1)
            total = total + dot(tok[:, i * 1024 : (i + 1) * 1024], rows)
        for i, h in enumerate(heads):
            raw = total[:, i * HEAD : (i + 1) * HEAD]
            keys[h] = (raw * cosine[...] + pltpu.roll(raw, half, 1) * sine[...]).astype(BF)

    def attend(h):
        acc[...] = jnp.zeros_like(acc)

        def one(g, _):
            lanes = pl.ds(pl.multiple_of((h * GROUP + g) * HEAD, HEAD), HEAD)
            queries = q[:, lanes]
            scores = dot_nt(keys[h], queries)
            parts = []
            for b in range(2):
                n = (b + 1) * 128
                span = slice(b * 128, (b + 1) * 128)
                s = scores[:n, span] + bias[:n, span]
                top = jnp.max(s, axis=0, keepdims=True)
                expo = jnp.exp2((s - top) * (SCALE * math.log2(math.e)))
                sl = SL[h * GROUP + g, b * 128 : b * 128 + n]
                norm = 1.0 / jnp.sum(expo, axis=0, keepdims=True)
                inner = jnp.sum(expo * sl, axis=0, keepdims=True) * norm
                parts.append((expo * (sl - inner) * (norm * SCALE)).astype(BF))
            low = jnp.concatenate([parts[0], jnp.zeros((128, 128), BF)], axis=0)
            dscores = jnp.concatenate([low, parts[1]], axis=1)
            acc[...] += dot(dscores, queries)
            return 0

        lax.fori_loop(0, GROUP, one, 0, unroll=8)

    def weight(h):
        total = acc[...]
        mine = (total * cosine[...] - pltpu.roll(total, half, 1) * sine[...]).astype(BF)
        gk[:, h * HEAD : (h + 1) * HEAD] = mine

        def give(i, _):
            eight = pl.ds(pl.multiple_of(i * 8, 8), 8)
            given = dot(TT[1, eight].reshape(512, TOK), mine)
            other[h, i] = given.astype(BF).reshape(2, 4, 64, HEAD)
            return 0

        lax.fori_loop(0, 4, give, 0, unroll=4)
        r0(h)

        def keep(i, _):
            eight = pl.ds(pl.multiple_of(i * 8, 8), 8)
            own[h, i] = dot(TT[0, eight].reshape(512, TOK), mine).reshape(2, 4, 64, HEAD)
            return 0

        lax.fori_loop(0, 4, keep, 0, unroll=4)

    def tokens_part(i, j):
        def one(n, _):
            rows = [W[h, n // 2, n % 2].reshape(512, HEAD) for h in range(HEADS)]
            cols = pl.ds(pl.multiple_of(n * 512, 512), 512)
            gt[:, cols] = dot_nt(gk[...], jnp.concatenate(rows, axis=1)).astype(BF)
            return 0

        lax.fori_loop(i, j, one, 0)

    to_core(0)
    slopes(3)
    for h in range(HEADS):
        project(h)
        if h == 0:
            to_core(1)
            to_core(2)
        elif h == 1:
            to_core(3)
        attend(h)
        if h >= 1:
            r1(h - 1)
        weight(h)

    def gather_sent():
        for p in range(2):
            for k in range(7):
                wait(mine[p], zs.at[p, k])
            for s in range(2):
                wait(first_slots(p, s), s1s.at[p, s])
        for h in range(HEADS):
            for s in range(2):
                wait(second_slots(h, s), s2s.at[h, s])
            wait(core_slice(h), cs.at[h])

    r2(0)
    r2(1)
    to_second(0)
    tokens_part(0, 1)
    r1(3)
    tokens_part(1, 5)
    r2(2)
    to_second(1)
    r3(0)
    tokens_part(5, 7)
    r2(3)
    to_second(2)
    tokens_part(7, 8)
    gather_sent()
    r3(1)
    r3(2)
    for h in range(HEADS):
        wait(RC.at[h], rcs.at[h])
        for s in range(2):
            wait(RA.at[h, s], ras.at[h, s])
    for n in range(3):
        for s in range(2):
            wait(RB.at[sets[n], s], rbs.at[n, s])
    r4(0)
    r4(1)
    r4(2)
    for n in range(3):
        wait(RZ.at[sets[n]], rzs.at[n])


def hand_over(gt, gw, gt_hbm, gw_hbm, sem):
    copies = [pltpu.make_async_copy(gw, gw_hbm, sem.at[4])]
    for i in range(4):
        rows = pl.ds(i * 64, 64)
        copies.append(pltpu.make_async_copy(gt.at[rows], gt_hbm.at[rows], sem.at[i]))
    for copy in copies:
        copy.start()
    for copy in copies:
        copy.wait()


def per_device(tokens, queries, values, upstream, key_weight, positions):
    inputs = (tokens, queries, values, upstream, key_weight, positions.reshape(1, TOK))
    far = pl.BlockSpec(memory_space=pltpu.HBM)
    near = pl.BlockSpec(memory_space=pltpu.VMEM)
    dma = pltpu.SemaphoreType.DMA
    vm = pltpu.VMEM
    results = pl.pallas_call(
        kernel,
        out_shape=(pltpu.VMEM((TOK, D), BF), pltpu.VMEM((16, HEADS * HEAD), F32)),
        in_specs=[far] * 6,
        out_specs=(near, near),
        scratch_shapes=[
            vm((HEADS * GROUP, 384, HEAD), F32),
            vm((TOK, D), BF), vm((TOK, D), BF), vm((TOK, HEADS * HEAD), BF), vm((TOK, D), BF),
            vm((16, HEADS * HEAD), BF), vm((1, TOK), jnp.int32),
            vm((HEADS, 4, 2, 4, 2, 4, 16, HEAD), BF),
            vm((2, 32, 64, TOK), BF),
            vm((TOK, HEAD), F32), vm((TOK, HEAD), F32), vm((TOK, TOK), F32),
            vm((HEADS, TOK, HEAD), BF), vm((TOK, HEAD), F32), vm((TOK, HEADS * HEAD), BF),
            vm((HEADS, 4, 2, 4, 64, HEAD), F32),
            vm((HEADS, 4, 2, 4, 64, HEAD), BF),
            vm((HEADS, 4, 2, 4, 64, HEAD), BF),
            vm((HEADS, 4, 2, 4, 64, HEAD), BF),
            vm((HEADS, 2, 3, 4, 64, HEAD), BF),
            vm((HEADS, 2, 4, 64, HEAD), F32),
            vm((HEADS, 2, 3, 64, HEAD), F32),
            vm((HEADS, 2, 4, 16, HEAD), F32),
            vm((HEADS, 7, 16, HEAD), F32),
            dma((6,)),
            dma((2, 7)), dma((2, 7)), dma((2, 2)), dma((2, 2)), dma((HEADS, 2)), dma((HEADS, 2)),
            dma((HEADS,)), dma((HEADS,)),
            dma((HEADS,)), dma((HEADS,)),
            dma((HEADS, 2)), dma((HEADS, 2)), dma((3, 2)), dma((3, 2)),
            dma((3,)), dma((3,)),
        ],
        compiler_params=pltpu.CompilerParams(
            collective_id=0, has_side_effects=True, vmem_limit_bytes=48 << 20
        ),
        cost_estimate=pl.CostEstimate(
            flops=5_000_000_000, bytes_accessed=9_000_000, transcendentals=2_000_000
        ),
        name="key_backward",
    )(*(pltpu.with_memory_space_constraint(a, pltpu.HBM) for a in inputs))
    return pl.pallas_call(
        hand_over,
        out_shape=(jax.ShapeDtypeStruct((TOK, D), BF), jax.ShapeDtypeStruct((16, HEADS * HEAD), F32)),
        in_specs=[near] * 2,
        out_specs=(far, far),
        scratch_shapes=[dma((5,))],
        name="hand_over",
    )(*(pltpu.with_memory_space_constraint(a, pltpu.VMEM) for a in results))


def solution(mesh):
    torus = Mesh(mesh.devices.reshape(4, 2, 4, 2, mesh.shape["local"]), AXES)
    rows = P(AXES, None)
    return jax.shard_map(
        per_device,
        mesh=torus,
        in_specs=(rows, rows, rows, rows, rows, P(AXES)),
        out_specs=(rows, rows),
        check_vma=False,
    )
```

```python
import math

import jax
import jax.numpy as jnp
from jax import lax
from jax.experimental import pallas as pl
from jax.experimental.pallas import tpu as pltpu
from jax.sharding import Mesh
from jax.sharding import PartitionSpec as P

AXES = ("y", "zh", "x", "c", "zl")
MESH = pl.DeviceIdType.MESH
HEADS = 4
GROUP = 8
HEAD = 128
TOK = 256
D = 4096
SCALE = HEAD**-0.5
BF = jnp.bfloat16
F32 = jnp.float32
FAR4 = (2, 1, 3)
FAR8 = (4, 3, 5, 2, 6, 1, 7)
NT = (((1,), (1,)), ((), ()))


def dot_nt(a, b):
    return lax.dot_general(a, b, NT, preferred_element_type=F32)


def dot(a, b):
    return jnp.dot(a, b, preferred_element_type=F32)


def kernel(
    tok_hbm, q_hbm, v_hbm, u_hbm, kw_hbm, pos_hbm,
    gt, gw_out,
    SL, tok, q, v, u, kw, pos, W, TT, cosine, sine, bias, keys, acc, gk,
    own, other, RC, A, RA, B, RB, C, RZ,
    load_sem,
    zs, zr, s1s, s1r, s2s, s2r, cs, cr,
    rcs, rcr, ras, rar, rbs, rbr, rzs, rzr,
):
    y, zh, x, c, zl = (lax.axis_index(a) for a in AXES)
    z = zh * 4 + zl
    other_core = (y, zh, x, 1 - c, zl)

    def at_x(k):
        return (y, zh, lax.rem(x + k, 4), c, zl)

    def at_y(k):
        return (lax.rem(y + k, 4), zh, x, c, zl)

    def at_z(k):
        there = lax.rem(z + k, 8)
        return (y, there // 4, x, c, lax.rem(there, 4))

    def send(src, dst, send_sem, recv_sem, where):
        pltpu.make_async_remote_copy(
            src_ref=src, dst_ref=dst, send_sem=send_sem, recv_sem=recv_sem,
            device_id=where, device_id_type=MESH,
        ).start()

    def wait(like, sem):
        pltpu.make_async_copy(like, like, sem).wait()

    barrier = pltpu.get_barrier_semaphore()
    peers = [at_z(k) for k in FAR8] + [f(k) for k in FAR4 for f in (at_x, at_y)] + [other_core]
    for peer in peers:
        pl.semaphore_signal(barrier, inc=1, device_id=peer, device_id_type=MESH)
    loads = [(kw_hbm, kw), (pos_hbm, pos), (tok_hbm, tok), (v_hbm, v), (q_hbm, q), (u_hbm, u)]
    copies = [pltpu.make_async_copy(a, b, load_sem.at[i]) for i, (a, b) in enumerate(loads)]
    for copy in copies:
        copy.start()
    copies[0].wait()
    for h in range(HEADS):
        W[h, y, zh, x, c, zl] = kw[:, h * HEAD : (h + 1) * HEAD]
    pl.semaphore_wait(barrier, len(peers))

    spans = (slice(0, 1), slice(1, HEADS))
    mine = [W.at[span, y, zh, x, c, zl] for span in spans]
    for p in range(2):
        for k in FAR8:
            send(mine[p], mine[p], zs.at[p, k - 1], zr.at[p, k - 1], at_z(k))

    copies[1].wait()
    lane = lax.broadcasted_iota(jnp.int32, (1, HEAD), 1)
    half = HEAD // 2
    freq = jnp.exp(-(lax.rem(lane, half).astype(F32) * 2.0 / HEAD) * math.log(1000000.0))
    place = pos[...].astype(F32)
    column = jnp.broadcast_to(place, (HEAD, TOK)).T
    angle = column * freq
    cosine[...] = jnp.cos(angle)
    sine[...] = jnp.where(lane < half, -1.0, 1.0) * jnp.sin(angle)
    row = lax.broadcasted_iota(jnp.int32, (TOK, TOK), 0)
    col = lax.broadcasted_iota(jnp.int32, (TOK, TOK), 1)
    allowed = (row <= col) & (row >= col - pos[...])
    bias[...] = jnp.where(allowed, 0.0, -1e30).astype(F32)

    copies[2].wait()

    def turn(i, _):
        block = tok[:, pl.ds(pl.multiple_of(i * HEAD, HEAD), HEAD)].T
        TT[c, i] = block[:64]
        TT[1 - c, i] = block[64:]
        return 0

    lax.fori_loop(0, 32, turn, 0)

    def slopes(h):
        def one(g, _):
            n = h * GROUP + g
            upper = u[:, pl.ds(pl.multiple_of(n * HEAD, HEAD), HEAD)]
            full = dot_nt(v[:, h * HEAD : (h + 1) * HEAD], upper)
            SL[n, :128] = full[:128, :128]
            SL[n, 128:] = full[:, 128:]
            return 0

        lax.fori_loop(0, GROUP, one, 0, unroll=4)

    def first_slice(p, s):
        return W.at[spans[p], y, s, x, c]

    def second_slice(h, s):
        return W.at[h, y, 0, :, c] if s == 0 else W.at[h, :, 1, x, c]

    def core_slice(h):
        return W.at[h, :, :, :, c]

    three = pl.ds(0, 3)

    def first_slots(p, s):
        return W.at[spans[p], y, s, three, c]

    def second_slots(h, s):
        return W.at[h, three, 0, :, c] if s == 0 else W.at[h, :, 1, three, c]

    def first_stage(p):
        for k in range(7):
            wait(mine[p], zr.at[p, k])
        for k in FAR4:
            for s in range(2):
                piece = first_slice(p, s)
                send(piece, piece, s1s.at[p, s], s1r.at[p, s], (at_x, at_y)[s](k))

    def second_stage(p):
        for s in range(2):
            wait(first_slots(p, s), s1r.at[p, s])
        for h in range(HEADS)[spans[p]]:
            for k in FAR4:
                for s in range(2):
                    piece = second_slice(h, s)
                    send(piece, piece, s2s.at[h, s], s2r.at[h, s], (at_y, at_x)[s](k))

    first_stage(0)
    first_stage(1)
    for copy in copies[3:]:
        copy.wait()
    slopes(0)
    second_stage(0)
    second_stage(1)
    slopes(1)
    slopes(2)

    def to_core(h):
        for s in range(2):
            wait(second_slots(h, s), s2r.at[h, s])
        send(core_slice(h), core_slice(h), cs.at[h], cr.at[h], other_core)

    def r0(h):
        send(other.at[h], RC.at[h], rcs.at[h], rcr.at[h], other_core)

    def r1(h):
        wait(RC.at[h], rcr.at[h])

        def add(i, _):
            A[h, i] = (own[h, i] + RC[h, i].astype(F32)).astype(BF)
            return 0

        lax.fori_loop(0, 4, add, 0)
        for k in FAR4:
            for s in range(2):
                piece = A.at[h, lax.rem(y + k, 4), 0] if s == 0 else A.at[h, :, 1, lax.rem(x + k, 4)]
                send(piece, RA.at[h, s, k - 1], ras.at[h, s], rar.at[h, s], (at_y, at_x)[s](k))

    def r2(h):
        for s in range(2):
            wait(RA.at[h, s], rar.at[h, s])
            total = (A[h, y, 0] if s == 0 else A[h, :, 1, x]).astype(F32)
            for k in range(3):
                total = total + RA[h, s, k].astype(F32)
            B[h, s] = total

    sets = (slice(0, 2), slice(2, 3), slice(3, 4))

    def to_second(n):
        for k in FAR4:
            for s in range(2):
                piece = B.at[sets[n], s, lax.rem((x, y)[s] + k, 4)]
                send(piece, RB.at[sets[n], s, k - 1], rbs.at[n, s], rbr.at[n, s], (at_x, at_y)[s](k))

    def r3(n):
        for s in range(2):
            wait(RB.at[sets[n], s], rbr.at[n, s])
            for h in range(HEADS)[sets[n]]:
                total = B[h, s, (x, y)[s]]
                for k in range(3):
                    total = total + RB[h, s, k]
                C[h, s] = total.reshape(4, 16, HEAD)
        for k in FAR8:
            there = lax.rem(z + k, 8)
            piece = C.at[sets[n], there // 4, lax.rem(there, 4)]
            send(piece, RZ.at[sets[n], k - 1], rzs.at[n], rzr.at[n], at_z(k))

    def r4(n):
        wait(RZ.at[sets[n]], rzr.at[n])
        for h in range(HEADS)[sets[n]]:
            total = C[h, zh, zl]
            for k in range(7):
                total = total + RZ[h, k]
            gw_out[:, h * HEAD : (h + 1) * HEAD] = total

    def project(*heads):
        for h in heads:
            wait(core_slice(h), cr.at[h])
        total = jnp.zeros((TOK, len(heads) * HEAD), F32)
        for i in range(4):
            rows = jnp.concatenate([W[h, i].reshape(1024, HEAD) for h in heads], axis=1)
            total = total + dot(tok[:, i * 1024 : (i + 1) * 1024], rows)
        for i, h in enumerate(heads):
            raw = total[:, i * HEAD : (i + 1) * HEAD]
            keys[h] = (raw * cosine[...] + pltpu.roll(raw, half, 1) * sine[...]).astype(BF)

    def attend(h):
        acc[...] = jnp.zeros_like(acc)

        def one(g, _):
            lanes = pl.ds(pl.multiple_of((h * GROUP + g) * HEAD, HEAD), HEAD)
            queries = q[:, lanes]
            scores = dot_nt(keys[h], queries)
            parts = []
            for b in range(2):
                n = (b + 1) * 128
                span = slice(b * 128, (b + 1) * 128)
                s = scores[:n, span] + bias[:n, span]
                top = jnp.max(s, axis=0, keepdims=True)
                expo = jnp.exp2((s - top) * (SCALE * math.log2(math.e)))
                sl = SL[h * GROUP + g, b * 128 : b * 128 + n]
                norm = 1.0 / jnp.sum(expo, axis=0, keepdims=True)
                inner = jnp.sum(expo * sl, axis=0, keepdims=True) * norm
                parts.append((expo * (sl - inner) * (norm * SCALE)).astype(BF))
            low = jnp.concatenate([parts[0], jnp.zeros((128, 128), BF)], axis=0)
            dscores = jnp.concatenate([low, parts[1]], axis=1)
            acc[...] += dot(dscores, queries)
            return 0

        lax.fori_loop(0, GROUP, one, 0, unroll=8)

    def weight(h):
        total = acc[...]
        mine = (total * cosine[...] - pltpu.roll(total, half, 1) * sine[...]).astype(BF)
        gk[:, h * HEAD : (h + 1) * HEAD] = mine

        def give(i, _):
            eight = pl.ds(pl.multiple_of(i * 8, 8), 8)
            given = dot(TT[1, eight].reshape(512, TOK), mine)
            other[h, i] = given.astype(BF).reshape(2, 4, 64, HEAD)
            return 0

        lax.fori_loop(0, 4, give, 0, unroll=4)
        r0(h)

        def keep(i, _):
            eight = pl.ds(pl.multiple_of(i * 8, 8), 8)
            own[h, i] = dot(TT[0, eight].reshape(512, TOK), mine).reshape(2, 4, 64, HEAD)
            return 0

        lax.fori_loop(0, 4, keep, 0, unroll=4)

    def tokens_part(i, j):
        def one(n, _):
            rows = [W[h, n // 2, n % 2].reshape(512, HEAD) for h in range(HEADS)]
            cols = pl.ds(pl.multiple_of(n * 512, 512), 512)
            gt[:, cols] = dot_nt(gk[...], jnp.concatenate(rows, axis=1)).astype(BF)
            return 0

        lax.fori_loop(i, j, one, 0)

    to_core(0)
    slopes(3)
    for h in range(HEADS):
        project(h)
        if h == 0:
            to_core(1)
            to_core(2)
        elif h == 1:
            to_core(3)
        attend(h)
        if h >= 1:
            r1(h - 1)
        weight(h)

    def gather_sent():
        for p in range(2):
            for k in range(7):
                wait(mine[p], zs.at[p, k])
            for s in range(2):
                wait(first_slots(p, s), s1s.at[p, s])
        for h in range(HEADS):
            for s in range(2):
                wait(second_slots(h, s), s2s.at[h, s])
            wait(core_slice(h), cs.at[h])

    r2(0)
    r2(1)
    to_second(0)
    r1(3)
    tokens_part(0, 5)
    r2(2)
    to_second(1)
    r3(0)
    tokens_part(5, 7)
    r2(3)
    to_second(2)
    tokens_part(7, 8)
    gather_sent()
    r3(1)
    r3(2)
    for h in range(HEADS):
        wait(RC.at[h], rcs.at[h])
        for s in range(2):
            wait(RA.at[h, s], ras.at[h, s])
    for n in range(3):
        for s in range(2):
            wait(RB.at[sets[n], s], rbs.at[n, s])
    r4(0)
    r4(1)
    r4(2)
    for n in range(3):
        wait(RZ.at[sets[n]], rzs.at[n])


def hand_over(gt, gw, gt_hbm, gw_hbm, sem):
    copies = [pltpu.make_async_copy(gw, gw_hbm, sem.at[4])]
    for i in range(4):
        rows = pl.ds(i * 64, 64)
        copies.append(pltpu.make_async_copy(gt.at[rows], gt_hbm.at[rows], sem.at[i]))
    for copy in copies:
        copy.start()
    for copy in copies:
        copy.wait()


def per_device(tokens, queries, values, upstream, key_weight, positions):
    inputs = (tokens, queries, values, upstream, key_weight, positions.reshape(1, TOK))
    far = pl.BlockSpec(memory_space=pltpu.HBM)
    near = pl.BlockSpec(memory_space=pltpu.VMEM)
    dma = pltpu.SemaphoreType.DMA
    vm = pltpu.VMEM
    results = pl.pallas_call(
        kernel,
        out_shape=(pltpu.VMEM((TOK, D), BF), pltpu.VMEM((16, HEADS * HEAD), F32)),
        in_specs=[far] * 6,
        out_specs=(near, near),
        scratch_shapes=[
            vm((HEADS * GROUP, 384, HEAD), F32),
            vm((TOK, D), BF), vm((TOK, D), BF), vm((TOK, HEADS * HEAD), BF), vm((TOK, D), BF),
            vm((16, HEADS * HEAD), BF), vm((1, TOK), jnp.int32),
            vm((HEADS, 4, 2, 4, 2, 4, 16, HEAD), BF),
            vm((2, 32, 64, TOK), BF),
            vm((TOK, HEAD), F32), vm((TOK, HEAD), F32), vm((TOK, TOK), F32),
            vm((HEADS, TOK, HEAD), BF), vm((TOK, HEAD), F32), vm((TOK, HEADS * HEAD), BF),
            vm((HEADS, 4, 2, 4, 64, HEAD), F32),
            vm((HEADS, 4, 2, 4, 64, HEAD), BF),
            vm((HEADS, 4, 2, 4, 64, HEAD), BF),
            vm((HEADS, 4, 2, 4, 64, HEAD), BF),
            vm((HEADS, 2, 3, 4, 64, HEAD), BF),
            vm((HEADS, 2, 4, 64, HEAD), F32),
            vm((HEADS, 2, 3, 64, HEAD), F32),
            vm((HEADS, 2, 4, 16, HEAD), F32),
            vm((HEADS, 7, 16, HEAD), F32),
            dma((6,)),
            dma((2, 7)), dma((2, 7)), dma((2, 2)), dma((2, 2)), dma((HEADS, 2)), dma((HEADS, 2)),
            dma((HEADS,)), dma((HEADS,)),
            dma((HEADS,)), dma((HEADS,)),
            dma((HEADS, 2)), dma((HEADS, 2)), dma((3, 2)), dma((3, 2)),
            dma((3,)), dma((3,)),
        ],
        compiler_params=pltpu.CompilerParams(
            collective_id=0, has_side_effects=True, vmem_limit_bytes=48 << 20
        ),
        cost_estimate=pl.CostEstimate(
            flops=5_000_000_000, bytes_accessed=9_000_000, transcendentals=2_000_000
        ),
        name="key_backward",
    )(*(pltpu.with_memory_space_constraint(a, pltpu.HBM) for a in inputs))
    return pl.pallas_call(
        hand_over,
        out_shape=(jax.ShapeDtypeStruct((TOK, D), BF), jax.ShapeDtypeStruct((16, HEADS * HEAD), F32)),
        in_specs=[near] * 2,
        out_specs=(far, far),
        scratch_shapes=[dma((5,))],
        name="hand_over",
    )(*(pltpu.with_memory_space_constraint(a, pltpu.VMEM) for a in results))


def solution(mesh):
    torus = Mesh(mesh.devices.reshape(4, 2, 4, 2, mesh.shape["local"]), AXES)
    rows = P(AXES, None)
    return jax.shard_map(
        per_device,
        mesh=torus,
        in_specs=(rows, rows, rows, rows, rows, P(AXES)),
        out_specs=(rows, rows),
        check_vma=False,
    )
```
